128 devices in a mesh: section: 2 (over core), shard: 16 (over y, z), replica: 4 (over x).
Axes of the slice: x: 4, y: 4, z: 4, core: 2. Of those that a mesh axis runs over, the one named last changes fastest.
Arguments:
- tokens: bfloat16 [8, 1024, 768], P('replica', 'shard'), may hold values from -6 to 6
- cotangent: bfloat16 [8, 1024, 768], P('replica', 'shard'), may hold values from -6 to 6
- query_key_value_weight: bfloat16 [2, 768, 2304], P('section', 'shard'), may hold values from -0.21875 to 0.21875
- attention_output_weight: bfloat16 [2, 768, 768], P('section', 'shard'), may hold values from -0.875 to 0.875
- gain_attn: bfloat16 [2, 768], P('section', 'shard'), may hold values from 0.5 to 1.5
- gain_ffn: bfloat16 [2, 768], P('section', 'shard'), may hold values from 0.5 to 1.5
- rel_table: bfloat16 [2, 32, 12], P('section', 'shard'), may hold values from -4 to 4
- w_in: bfloat16 [2, 64, 768, 3072], P('section', ('shard', 'replica')), may hold values from -0.21875 to 0.21875
- w_out_exp: bfloat16 [2, 64, 3072, 768], P('section', ('shard', 'replica')), may hold values from -0.109375 to 0.109375
- expert_ids: int32 [2, 8, 1024, 2], P('section', 'replica', 'shard'), may hold values from 0 to 63, all different within a row; in each aligned block of 64 rows (0 to 63, 64 to 127, ..., all dimensions but the last counted through in order) at most 3 rows name the same one
- gates: float32 [2, 8, 1024, 2], P('section', 'replica', 'shard'), may hold values from 0.2 to 0.8
- seg_ids: int32 [8, 1024], P('replica'), may hold values from 0 to 3, as said below
- buckets: int32 [1024], replicated, may hold values from 0 to 31, as said below
Outputs:
- activations: bfloat16 [2, 8, 1024, 768], P('section', 'replica', 'shard')
- section_grads: bfloat16 [2, 8, 1024, 768], P('section', 'replica', 'shard')
- grad_qkv: bfloat16 [2, 768, 2304], P('section', 'shard')
- grad_attn_out: bfloat16 [2, 768, 768], P('section', 'shard')
- grad_gain_attn: bfloat16 [2, 768], P('section', 'shard')
- grad_gain_ffn: bfloat16 [2, 768], P('section', 'shard')
- grad_table: bfloat16 [2, 32, 12], P('section', 'shard')
- grad_w_in: bfloat16 [2, 64, 768, 3072], P('section', ('shard', 'replica'))
- grad_w_out_exp: bfloat16 [2, 64, 3072, 768], P('section', ('shard', 'replica'))
The draws below stay inside these ranges and needn't reach their ends.
Inputs may be any that keep to these rules, and one draw needn't show every extreme that they name: `seg_ids`: within a sequence the document number starts at 0 and never falls; of the 2 sequences of each replica group one is a single document. The bucket of distance 0 is 0, buckets never fall as the distance grows, and every bucket occurs. `expert_ids`: each token names two different experts; within each aligned block of 64 tokens of a sequence no expert is named more than 3 times.
All inputs are finite; a program needn't handle non-finite values.
Results may differ from the reference program's by a relative error of at most 0.028.
Values may be sent and summed in bfloat16 or wider, within the bound.
A program may use at most 192 MiB of HBM per device.

```python
import math
import jax
import jax.numpy as jnp
import numpy as np
from jax import lax

D = 768
HEADS = 12
FF = 3072
BUCKETS = 32
LENGTH = 1024
MB = 2
EXPERTS = 64
ROWS = 64
CAP = 3
SEQS = 8
N_SECTION = 2
N_SHARD = 16


def draw_seg_ids(key, part):
    key = jax.random.fold_in(key, 11)
    whole_key, cut_key = jax.random.split(key)
    chosen = jax.random.randint(whole_key, (SEQS // MB,), 0, MB)
    row_index = jnp.arange(SEQS)
    single_doc = row_index % MB == chosen[row_index // MB]

    def cuts_of(one_key):
        return jnp.sort(jax.random.permutation(one_key, LENGTH - 1)[:3] + 1)
    cut_points = jax.vmap(cuts_of)(jax.random.split(cut_key, SEQS))
    positions = jnp.arange(LENGTH)
    doc_ids = jnp.sum((positions[None, :, None] >= cut_points[:, None, :]).astype(jnp.int32), axis=2)
    return jnp.where(single_doc[:, None], 0, doc_ids).astype(jnp.int32)


def draw_buckets(key, part):
    key = jax.random.fold_in(key, 23)
    break_points = jnp.sort(jax.random.permutation(key, LENGTH - 1)[:BUCKETS - 1] + 1)
    distance = jnp.arange(LENGTH)
    return jnp.sum((distance[:, None] >= break_points[None, :]).astype(jnp.int32), axis=1).astype(jnp.int32)


def block_levels(own_key, extent, cuts, smallest, largest):
    loudness = 1.0
    for axis_at, shards_of in cuts:
        draws = jax.random.uniform(jax.random.fold_in(jax.random.fold_in(own_key, 6), axis_at), (shards_of,), jnp.float32, smallest / len(cuts), largest / len(cuts))
        loudness = loudness * jnp.repeat(jnp.exp(draws), extent[axis_at] // shards_of).reshape((-1,) + (1,) * (len(extent) - 1 - axis_at))
    return loudness


def deal_out(stream_key, own, number, rows, count, top, limit, slope):
    order = jax.random.permutation(stream_key, count)
    crowded, common = load_shares(count, rows * top, limit, slope, True), load_shares(count, rows * top, limit, slope, False)
    places = jnp.arange(count)

    def named(sizes, rotation):
        used = int((sizes > 0).sum())
        fixed = max(1, used // 4)
        shifted = fixed + (places - fixed + rotation * (used - fixed)) % max(1, count - fixed)
        return jnp.zeros((count,), jnp.int32).at[order[jnp.where(places < fixed, places, shifted)]].set(jnp.asarray(sizes, jnp.int32))

    sizes = jnp.where(number % 4 == 0, named(crowded, number // 4), named(common, number - number // 4 - 1))
    mixed = jax.random.permutation(jax.random.fold_in(own, 3), count)
    donor, taker = mixed[0:count // 2 * 2:2], mixed[1:count // 2 * 2:2]
    slack = jnp.minimum(sizes[donor] - 1, limit - sizes[taker]) // 2
    slack = jnp.where((donor == order[0]) | (taker == order[0]) | (sizes[taker] == 0), 0, jnp.maximum(slack, 0))
    shifted = jax.random.randint(jax.random.fold_in(own, 4), (count // 2,), 0, 1 << 20) % (slack + 1)
    sizes = sizes.at[donor].add(-shifted).at[taker].add(shifted)
    labels = jnp.searchsorted(jnp.cumsum(sizes), jnp.arange(rows * top), side="right").astype(jnp.int32)
    listing = labels.reshape(top, rows).T
    listing = listing[jax.random.permutation(jax.random.fold_in(own, 1), rows)]
    rotation = jax.random.randint(jax.random.fold_in(own, 2), (rows, 1), 0, top)
    return jnp.take_along_axis(listing, (jnp.arange(top)[None, :] + rotation) % top, axis=1)


def load_shares(count, total, most, lean, full):
    loads = [(1 << 20) // math.isqrt(grade ** lean) + 1 for grade in range(1, count + 1)]
    largest = most if full else min(most, max(-(-total // count), total * loads[0] // sum(loads)))
    least = 1 if total - largest >= count - 1 else 0
    given, rest = [largest] + [least] * (count - 1), total - largest - least * (count - 1)
    while rest > 0:
        free = [i for i in range(1, count) if given[i] < largest] or [i for i in range(1, count) if given[i] < most]
        mass, budget = sum([loads[i] for i in free]), rest
        for i in free:
            extra = min(most - given[i], max(1, budget * loads[i] // mass), rest)
            given[i] = given[i] + extra
            rest = rest - extra
    return np.array(given)


def scatter_about(key, shape, width, bound, cuts=(), dtype=jnp.bfloat16):
    result = jax.random.normal(key, shape, jnp.float32) * width
    if len(cuts) > 0:
        result = block_levels(key, shape, cuts, -0.22, 0.18) * result
    return jnp.clip(result, min=-bound, max=bound).astype(dtype)


def setup_inputs(seed: int = 0) -> dict:
    seeds = jax.random.split(jax.random.key(seed), 14)
    tokens = scatter_about(seeds[0], (SEQS, LENGTH, D), 1.0, 6.0, ((0, 4), (1, 16)))
    cotangent = scatter_about(seeds[1], (SEQS, LENGTH, D), 1.0, 6.0, ((0, 4), (1, 16)))
    query_key_value_weight = scatter_about(seeds[2], (N_SECTION, D, 3 * D), D ** -0.5, 0.21875, ((0, 2), (1, 16)))
    attention_output_weight = scatter_about(seeds[3], (N_SECTION, D, D), (D // 16) ** -0.5, 0.875, ((0, 2), (1, 16)))
    gain_attn = jnp.clip(1.0 + 0.1 * jax.random.normal(seeds[4], (N_SECTION, D), jnp.float32), 0.5, 1.5).astype(jnp.bfloat16)
    gain_ffn = jnp.clip(1.0 + 0.1 * jax.random.normal(seeds[5], (N_SECTION, D), jnp.float32), 0.5, 1.5).astype(jnp.bfloat16)
    rel_table = scatter_about(seeds[6], (N_SECTION, BUCKETS, HEADS), 1.0, 4.0, ((0, 2), (1, 16)))
    w_in = scatter_about(seeds[7], (N_SECTION, EXPERTS, D, FF), D ** -0.5, 0.21875, ((0, 2), (1, 64)))
    w_out_exp = scatter_about(seeds[8], (N_SECTION, EXPERTS, FF, D), FF ** -0.5, 0.109375, ((0, 2), (1, 64)))
    expert_ids_keys = jax.random.split(jax.random.fold_in(seeds[9], 1), N_SECTION * SEQS * LENGTH // ROWS)
    expert_ids_turns = jax.random.permutation(jax.random.fold_in(seeds[9], 3), N_SECTION * SEQS * LENGTH // ROWS)
    expert_ids = jax.vmap(lambda own, number: deal_out(jax.random.fold_in(seeds[9], 2), own, number, ROWS, EXPERTS, 2, CAP, 1))(expert_ids_keys, expert_ids_turns).reshape((N_SECTION, SEQS, LENGTH, 2))
    gates = jnp.clip(0.2 + 0.6 * jax.random.uniform(seeds[10], (N_SECTION, SEQS, LENGTH, 2), jnp.float32) ** block_levels(seeds[10], (N_SECTION, SEQS, LENGTH, 2), ((0, 2), (1, 4), (2, 16)), -0.2, 0.2), 0.2, 0.8)
    seg_ids = draw_seg_ids(jax.random.fold_in(seeds[13], 71), 0)
    buckets = draw_buckets(jax.random.fold_in(seeds[13], 71), 0)
    return dict(tokens=tokens, cotangent=cotangent, query_key_value_weight=query_key_value_weight, attention_output_weight=attention_output_weight, gain_attn=gain_attn, gain_ffn=gain_ffn, rel_table=rel_table, w_in=w_in, w_out_exp=w_out_exp, expert_ids=expert_ids, gates=gates, seg_ids=seg_ids, buckets=buckets)


@jax.custom_vjp
def low(v):
    return lax.optimization_barrier(v.astype(jnp.bfloat16)).astype(jnp.float32)

@jax.custom_vjp
def lower_reverse_pass(v):
    return v

def low_keep(v):
    return (low(v), None)

def low_pass(kept, grad):
    return (grad,)

def back_keep(v):
    return (v, None)

def back_low(kept, grad):
    return (low(grad),)
low.defvjp(low_keep, low_pass)
lower_reverse_pass.defvjp(back_keep, back_low)
peak_score = lax.Precision.HIGHEST

def norm_piece(inputs, gain_vec):
    return inputs * lax.rsqrt(lax.optimization_barrier(jnp.mean(inputs * inputs, axis=-1, keepdims=True)) + 1e-06) * gain_vec

def attend_one(queries, keys_all, values_all, seg_row, relative_position_bias):
    raw_scores = lower_reverse_pass(jnp.einsum('qhd,khd->hqk', queries, keys_all, precision=peak_score) * 0.125)
    positions = jnp.arange(queries.shape[0]).astype(jnp.int32)
    allowed = (positions[None, :] <= positions[:, None]) & (seg_row[:, None] == seg_row[None, :])
    logits = jnp.where(allowed[None], raw_scores + relative_position_bias, -1e+30)
    attn_probs = low(jax.nn.softmax(logits, axis=-1))
    return jnp.einsum('hqk,khd->qhd', attn_probs, values_all, precision=peak_score)

def layer(inputs, query_key_value_weight, attention_output_weight, gain_attn, gain_ffn, rel_table, w_in, w_out_exp, expert_ids, gates, seg_ids, buckets):
    seq_count, seq_length, model_width = inputs.shape
    head_count = rel_table.shape[1]
    head_dim = model_width // head_count
    expert_count = w_in.shape[0]
    normalized_input = low(norm_piece(inputs, gain_attn))
    query_key_value = jnp.einsum('zix,xm->zim', normalized_input, query_key_value_weight, precision=peak_score)
    shape_four = (seq_count, seq_length, head_count, head_dim)
    queries = lower_reverse_pass(low(query_key_value[..., :model_width])).reshape(shape_four)
    keys_all = lower_reverse_pass(low(query_key_value[..., model_width:2 * model_width])).reshape(shape_four)
    values_all = lower_reverse_pass(low(query_key_value[..., 2 * model_width:])).reshape(shape_four)
    positions = jnp.arange(seq_length).astype(jnp.int32)
    distance = jnp.maximum(positions[:, None] - positions[None, :], 0).astype(jnp.int32)
    relative_position_bias = jnp.transpose(rel_table[buckets[distance]], (2, 0, 1))

    def attend_member(member):
        return attend_one(member[0], member[1], member[2], member[3], relative_position_bias)
    mixed_heads_output = lax.map(jax.checkpoint(attend_member), (queries, keys_all, values_all, seg_ids))
    mixed_heads_output = lower_reverse_pass(low(mixed_heads_output.reshape(seq_count, seq_length, model_width)))
    attention_result = lower_reverse_pass(jnp.einsum('zix,xm->zim', mixed_heads_output, attention_output_weight, precision=peak_score))
    hidden = inputs + attention_result
    normed_two = low(norm_piece(hidden, gain_ffn)).reshape(-1, model_width)
    token_count = normed_two.shape[0]
    padded = jnp.concatenate([normed_two, jnp.zeros((1, model_width), jnp.float32)], 0)
    flat_ids = expert_ids.reshape(-1).astype(jnp.int32)
    indicator_matrix = (flat_ids[:, None] == jnp.arange(expert_count).astype(jnp.int32)[None, :]).astype(jnp.int32)
    slot_rank = lax.optimization_barrier(jnp.sum((jnp.cumsum(indicator_matrix, axis=0) - 1) * indicator_matrix, axis=1)).astype(jnp.int32)
    slots_each = SEQS * N_SHARD * CAP
    slot_index = (flat_ids * slots_each + slot_rank).astype(jnp.int32)
    token_of = (jnp.arange(2 * token_count) // 2).astype(jnp.int32)
    slot_owner = jnp.full((expert_count * slots_each,), token_count, jnp.int32).at[slot_index].set(token_of)
    expert_rows = lower_reverse_pass(padded[slot_owner]).reshape(expert_count, slots_each, model_width)
    pre_act = lower_reverse_pass(jnp.einsum('esd,edf->esf', expert_rows, w_in, precision=peak_score))
    gelu_out = low(jax.nn.gelu(pre_act))
    out_rows = lower_reverse_pass(low(jnp.einsum('esf,efd->esd', gelu_out, w_out_exp, precision=peak_score)))
    picked = out_rows.reshape(-1, model_width)[slot_index].reshape(token_count, 2, model_width)
    expert_sum = lax.optimization_barrier(jnp.sum(gates.reshape(token_count, 2, 1) * picked, axis=1))
    return hidden + expert_sum.reshape(seq_count, seq_length, model_width)

def to_float(array):
    return array.astype(jnp.float32)

def reference(tokens, cotangent, query_key_value_weight, attention_output_weight, gain_attn, gain_ffn, rel_table, w_in, w_out_exp, expert_ids, gates, seg_ids, buckets):

    def params_of(index):
        return tuple((to_float(array[index]) for array in (query_key_value_weight, attention_output_weight, gain_attn, gain_ffn, rel_table, w_in, w_out_exp)))

    def section_fn(index):

        def run_layer(inputs, *weights):
            return layer(inputs, *weights, expert_ids[index], gates[index], seg_ids, buckets)
        return run_layer
    first_out, first_vjp = jax.vjp(section_fn(0), to_float(tokens), *params_of(0))
    passed = first_out.astype(jnp.bfloat16)
    final_out, second_vjp = jax.vjp(section_fn(1), to_float(passed), *params_of(1))
    second_grads = second_vjp(to_float(cotangent))
    returned = second_grads[0].astype(jnp.bfloat16)
    first_grads = first_vjp(to_float(returned))
    activations = jnp.stack([passed, final_out.astype(jnp.bfloat16)])
    section_grads = jnp.stack([first_grads[0].astype(jnp.bfloat16), returned])
    stacked = [jnp.stack([first_grads[index], second_grads[index]]).astype(jnp.bfloat16) for index in range(1, 8)]
    return (activations, section_grads, stacked[0], stacked[1], stacked[2], stacked[3], stacked[4], stacked[5], stacked[6])
```

```python
import jax
import jax.numpy as jnp
from jax import lax
from jax.experimental import pallas as pl
from jax.experimental.pallas import tpu as pltpu
from jax.sharding import PartitionSpec as P

MESH = pl.DeviceIdType.MESH
F32 = jnp.float32
BF16 = jnp.bfloat16
HIGH = lax.Precision.HIGHEST

D, HEADS, HD, FF = 768, 12, 64, 3072
LENGTH, ROWS, EXPERTS, SLOTS = 1024, 64, 64, 8
SHARDS, REPLICAS = 16, 4
TOK = 2 * ROWS
SLOT_ROWS = EXPERTS * SLOTS
BAND = LENGTH + 128
TILE = 256
C0 = 0.7978845608028654
C1 = C0 * 0.044715

MISC, GA1, GB1, GA2, GB2 = 0, 1, 2, 3, 4
QKV, MIX, DOUT, DQKV = 6, 8, 10, 12
DISP, RET, DY, DEXP, XPASS, GPASS = 14, 15, 16, 17, 18, 19
GTAB, SMALL, GW, GX, SX = 20, 21, 22, 23, 24
WIN, WOUT, OWIN, OWOUT = 25, 26, 27, 28

SCRATCH = dict(
    ga=((4, 4, 48, 1536), BF16),
    gb=((4, 4, 48, 1536), BF16),
    mr=((32, 8, 128), F32),
    gains=((8, D), F32),
    tb=((2, 128, LENGTH), F32),
    gg=((128, BAND), F32),
    win=((D, FF), BF16),
    wout=((FF, D), BF16),
    qs=((24, 64, 256), BF16),
    qr=((2, 16, 64, 256), BF16),
    os=((2, 16, 64, 128), BF16),
    mx=((24, 64, 128), BF16),
    mixed=((TOK, D), BF16),
    nrm=((TOK, D), BF16),
    hidden=((TOK, D), F32),
    xsend=((TOK, D), BF16),
    xin=((TOK, D), BF16),
    gin=((TOK, D), BF16),
    ds=((EXPERTS, SLOTS, D), BF16),
    dr=((EXPERTS, SLOTS, D), BF16),
    rs=((EXPERTS, SLOTS, D), BF16),
    rr=((EXPERTS, SLOTS, D), BF16),
    ys=((EXPERTS, SLOTS, D), BF16),
    yr=((EXPERTS, SLOTS, D), BF16),
    es=((EXPERTS, SLOTS, D), BF16),
    er=((EXPERTS, SLOTS, D), BF16),
    rows=((SLOT_ROWS, D), BF16),
    dyrows=((SLOT_ROWS, D), BF16),
    act=((SLOT_ROWS, FF), BF16),
    dg=((SLOT_ROWS, FF), BF16),
    acc=((SLOT_ROWS, D), F32),
    lse=((2, LENGTH, 1), F32),
    dos=((24, 64, 128), BF16),
    dor=((2, 16, 64, 128), BF16),
    dks=((2, 16, 64, 256), BF16),
    dkr=((24, 64, 256), BF16),
    dkv=((LENGTH, 128), F32),
    dqk=((TOK, 1536), BF16),
    dvv=((TOK, D), BF16),
    dh=((TOK, D), F32),
    gp=((16, 48, 3072), BF16),
    gr=((16, 48, 3072), BF16),
    gxs=((48, 3072), BF16),
    gx=((4, 48, 3072), BF16),
    sm=((8, D), F32),
    smr=((16, 8, D), F32),
    sxs=((8, D), F32),
    sx=((4, 8, D), F32),
    gts=((2, 8, 128), F32),
    gtr=((24, 8, 128), F32),
)
INPUTS = ("tok", "cot", "wcat", "misc", "oh", "segr", "segc", "smat", "stmat", "gh", "gl", "gth", "gtl", "winh", "wouth")
OUTPUTS = ("acts", "sgr", "gwo", "smo", "gwin", "gwout")


def dot(a, b, **kw):
    return jnp.dot(a, b, preferred_element_type=F32, **kw)


def dot_nt(a, b, **kw):
    return lax.dot_general(a, b, (((1,), (1,)), ((), ())), preferred_element_type=F32, **kw)


def dot_tn(a, b, **kw):
    return lax.dot_general(a, b, (((0,), (0,)), ((), ())), preferred_element_type=F32, **kw)


def loop(count, step):
    def wrapped(i, carry):
        step(i)
        return carry
    lax.fori_loop(0, count, wrapped, 0)


def kernel(*refs):
    names = INPUTS + OUTPUTS + tuple(SCRATCH) + ("ssem", "rsem")
    R = dict(zip(names, refs))
    ssem, rsem = R["ssem"], R["rsem"]
    c = lax.axis_index("section")
    s = lax.axis_index("shard")
    r = lax.axis_index("replica")
    e = s * REPLICAS + r
    y = s // 4
    z = s % 4

    def push(src, dst, i, tc, ts, tr):
        same = (tc == c) & (ts == s) & (tr == r)

        @pl.when(same)
        def _():
            pltpu.make_async_copy(src, dst, rsem.at[i]).start()

        @pl.when(jnp.logical_not(same))
        def _():
            send(src, dst, i, tc, ts, tr)

    def send(src, dst, i, tc, ts, tr):
        pltpu.make_async_remote_copy(
            src_ref=src, dst_ref=dst, send_sem=ssem.at[i], recv_sem=rsem.at[i],
            device_id=(tc, ts, tr), device_id_type=MESH,
        ).start()

    def got(ref, i):
        pltpu.make_async_copy(ref, ref, rsem.at[i]).wait()

    def sent(ref, i):
        pltpu.make_async_copy(ref, ref, ssem.at[i]).wait()

    pltpu.make_async_copy(R["winh"], R["win"], rsem.at[WIN]).start()
    pltpu.make_async_copy(R["wouth"], R["wout"], rsem.at[WOUT]).start()

    def misc_step(i):
        push(R["misc"], R["mr"].at[c * 16 + s], MISC, i // 16, i % 16, r)
    loop(32, misc_step)

    wcat, ga, gb = R["wcat"], R["ga"], R["gb"]

    def gather_one(i):
        push(wcat.at[:, pl.ds(0, 1536)], ga.at[y, z], GA1, c, y * 4 + i, r)
        push(wcat.at[:, pl.ds(1536, 1536)], gb.at[y, z], GB1, c, i * 4 + z, r)
    loop(4, gather_one)
    got(ga.at[y], GA1)
    got(gb.at[:, z], GB1)

    def gather_two(i):
        @pl.when(i != y)
        def _():
            send(ga.at[y], ga.at[y], GA2, c, i * 4 + z, r)

        @pl.when(i != z)
        def _():
            send(gb.at[:, z], gb.at[:, z], GB2, c, y * 4 + i, r)
    loop(4, gather_two)

    got(R["mr"], MISC)
    mr = R["mr"]
    lane = lax.broadcasted_iota(jnp.int32, (8, D), 1)
    total = jnp.zeros((8, D), F32)
    for k in range(SHARDS):
        piece = jnp.concatenate([mr[c * 16 + k], jnp.zeros((8, D - 128), F32)], axis=1)
        piece = jnp.where(lane < 48, piece, 0.0)
        total = total + (pltpu.roll(piece, 48 * k, 1) if k else piece)
    R["gains"][...] = total

    is_head = s < HEADS

    @pl.when(is_head)
    def _():
        sub = lax.broadcasted_iota(jnp.int32, (8, 128), 0)
        for l in range(2):
            tab = jnp.zeros((8, 128), F32)
            for k in range(SHARDS):
                tab = tab + (pltpu.roll(mr[l * 16 + k], 2 * k, 1) if k else mr[l * 16 + k])
            tab = jnp.where(sub == 2 + s // 2, tab, 0.0)
            tab = pltpu.roll(tab, (s % 2) * 64, 1)
            row = jnp.sum(tab, axis=0, keepdims=True)
            base = dot(jnp.broadcast_to(row, (8, 128)).astype(BF16), R["oh"][...])
            band = jnp.broadcast_to(base[0:1], (128, BAND))
            band = pltpu.roll(band, BAND - 127, 1, stride=1, stride_axis=0)
            R["tb"][l] = band[:, :LENGTH]

    got(ga.at[pl.ds(0, 3)], GA2)
    got(gb.at[pl.ds(0, 3)], GB2)

    def head_parts(l):
        both = R["qr"][l].reshape(LENGTH, 256)
        return both[:, 0:64], both[:, 64:128], both[:, 128:192] * BF16(0.125)

    def logits(l, b, q, keys):
        nk = 128 * (b + 1)
        scores = dot_nt(q[128 * b:nk], keys[:nk]) + R["tb"][l, :, 896 - 128 * b:1024]
        row = lax.broadcasted_iota(jnp.int32, (128, nk), 0) + 128 * b
        col = lax.broadcasted_iota(jnp.int32, (128, nk), 1)
        ok = (col <= row) & (R["segc"][128 * b:nk, :] == R["segr"][:, :nk])
        return jnp.where(ok, scores, -1e30)

    def head_fwd(l):
        got(R["qr"].at[l], QKV + l)
        keys, values, q = head_parts(l)
        for b in range(8):
            nk = 128 * (b + 1)
            lg = logits(l, b, q, keys)
            top = jnp.max(lg, axis=1, keepdims=True)
            ex = jnp.exp(lg - top)
            tot = jnp.sum(ex, axis=1, keepdims=True)
            out = dot(ex.astype(BF16), values[:nk]) / tot
            R["os"][l, 2 * b:2 * b + 2, :, 0:64] = out.astype(BF16).reshape(2, 64, 64)
            R["lse"][l, 128 * b:nk, :] = top + jnp.log(tot)

        def back(i):
            push(R["os"].at[l, i], R["mx"].at[c * HEADS + s], MIX + l, l, i, r)
        loop(SHARDS, back)

    def head_bwd(l):
        got(R["dor"].at[l], DOUT + l)
        keys, values, q = head_parts(l)
        dor, dks, dkv, gg = R["dor"], R["dks"], R["dkv"], R["gg"]
        dkv[...] = jnp.zeros(dkv.shape, F32)
        gg[...] = jnp.zeros(gg.shape, F32)
        for b in range(8):
            nk = 128 * (b + 1)
            qb = q[128 * b:nk]
            prob = jnp.exp(logits(l, b, q, keys) - R["lse"][l, 128 * b:nk, :])
            do = dor[l, 2 * b:2 * b + 2, :, 0:64].reshape(128, 64)
            dp = dot_nt(do, values[:nk])
            delta = jnp.sum(prob * dp, axis=1, keepdims=True)
            dlog = prob * (dp - delta)
            gg[:, 896 - 128 * b:1024] += dlog
            low = dlog.astype(BF16)
            dq = dot(low, keys[:nk]) * 0.125
            dks[l, 2 * b:2 * b + 2, :, 128:192] = dq.astype(BF16).reshape(2, 64, 64)
            dkv[:nk, 0:64] += dot_tn(low, qb)
            dkv[:nk, 64:128] += dot_tn(prob.astype(BF16), do)
        dks[l, :, :, 0:128] = dkv[...].astype(BF16).reshape(16, 64, 128)

        def back(i):
            push(dks.at[l, i], R["dkr"].at[c * HEADS + s], DQKV + l, l, i, r)
        loop(SHARDS, back)
        flip = (lax.broadcasted_iota(jnp.int32, (128, 128), 0) + lax.broadcasted_iota(jnp.int32, (128, 128), 1)) == 127
        band = dot(flip.astype(F32), gg[...], precision=HIGH)
        band = pltpu.roll(band, 0, 1, stride=1, stride_axis=0)
        diag = jnp.sum(band, axis=0, keepdims=True)
        tg = dot_nt(jnp.broadcast_to(diag, (8, BAND)), R["oh"][...].astype(F32), precision=HIGH)
        sub = lax.broadcasted_iota(jnp.int32, (8, 128), 0)
        tg = jnp.where(sub == 2 + s // 2, pltpu.roll(tg, (s % 2) * 64, 1), 0.0)
        R["gts"][l] = tg

        def back_table(i):
            push(R["gts"].at[l], R["gtr"].at[c * HEADS + s], GTAB, l, i, r)
        loop(SHARDS, back_table)

    def norm(x):
        return x * lax.rsqrt(jnp.mean(x * x, axis=1, keepdims=True) + 1e-06)

    def norm_back(x, gain, dn):
        rstd = lax.rsqrt(jnp.mean(x * x, axis=1, keepdims=True) + 1e-06)
        n = x * rstd
        dgain = jnp.sum(dn * n, axis=0, keepdims=True)
        dng = dn * gain
        return rstd * (dng - n * jnp.mean(dng * n, axis=1, keepdims=True)), dgain

    def spread(buf, dst, i, l):
        def step(k):
            push(buf.at[k], dst.at[e], i, l, k // REPLICAS, k % REPLICAS)
        loop(EXPERTS, step)

    def slots(value):
        return value.reshape(EXPERTS, SLOTS, D).astype(BF16)

    def flat(ref):
        return ref[...].astype(F32).reshape(SLOT_ROWS, D).astype(BF16)

    def to_heads(buf, dst, i):
        def step(u):
            push(buf.at[u], dst.at[s], i, u // HEADS, u % HEADS, r)
        loop(24, step)

    def tile(t):
        return pl.ds(pl.multiple_of(t * TILE, TILE), TILE)

    def layer_in(l):
        return R["tok"][...] if l == 0 else R["xin"][...]

    def wk():
        return ga[...].reshape(D, 1536)

    def wv():
        return gb[:, :, :, 0:D].reshape(D, D)

    def wo():
        return gb[:, :, :, D:2 * D].reshape(D, D)

    def fwd_one(l):
        if l == 1:
            got(R["xin"], XPASS)
        x = layer_in(l).astype(F32)
        nrm = (norm(x) * R["gains"][0:1, :]).astype(BF16)
        R["nrm"][...] = nrm
        qk = dot(nrm, wk()).astype(BF16)
        v = dot(nrm, wv()).astype(BF16)
        qs = R["qs"]
        for u in range(24):
            rows = slice(64 * (u // HEADS), 64 * (u // HEADS) + 64)
            h = 64 * (u % HEADS)
            qs[u, :, 0:64] = qk[rows, D + h:D + h + 64]
            qs[u, :, 64:128] = v[rows, h:h + 64]
            qs[u, :, 128:192] = qk[rows, h:h + 64]
        to_heads(qs, R["qr"].at[l], QKV + l)

    def fwd_two(l):
        got(R["mx"], MIX + l)
        mx, mixed = R["mx"], R["mixed"]
        for u in range(24):
            rows = slice(64 * (u // HEADS), 64 * (u // HEADS) + 64)
            h = 64 * (u % HEADS)
            mixed[rows, h:h + 64] = mx[u, :, 0:64]
        hidden = layer_in(l).astype(F32) + dot(mixed[...], wo())
        R["hidden"][...] = hidden
        nrm2 = (norm(hidden) * R["gains"][1:2, :]).astype(BF16)
        R["ds"][...] = slots(dot(R["smat"][...], nrm2))
        spread(R["ds"], R["dr"], DISP, l)

        got(R["win"], WIN)
        got(R["wout"], WOUT)
        got(R["dr"], DISP)
        rows, acc, win, wout = R["rows"], R["acc"], R["win"], R["wout"]
        rows[...] = flat(R["dr"])
        acc[...] = jnp.zeros(acc.shape, F32)

        def ffn(t):
            at = tile(t)
            pre = dot(rows[...], win[:, at])
            sq = pre * pre
            th = jnp.tanh(pre * (C0 + C1 * sq))
            half = 0.5 * (1.0 + th)
            act = (pre * half).astype(BF16)
            R["act"][:, at] = act
            R["dg"][:, at] = (half + 0.5 * pre * (1.0 - th * th) * (C0 + 3.0 * C1 * sq)).astype(BF16)
            acc[...] += dot(act, wout[at, :])
        loop(FF // TILE, ffn)
        R["rs"][...] = slots(acc[...])
        spread(R["rs"], R["rr"], RET, l)
        got(R["rr"], RET)
        back = flat(R["rr"])
        out = R["hidden"][...] + dot(R["gth"][...], back) + dot(R["gtl"][...], back)
        R["acts"][...] = out.astype(BF16)
        if l == 0:
            R["xsend"][...] = out.astype(BF16)
            send(R["xsend"], R["xin"], XPASS, 1, s, r)

    def bwd_one(l):
        if l == 0:
            got(R["gin"], GPASS)
        g = R["cot"][...] if l == 1 else R["gin"][...]
        R["ys"][...] = slots(dot(R["gh"][...], g) + dot(R["gl"][...], g))
        spread(R["ys"], R["yr"], DY, l)
        got(R["yr"], DY)
        rows, acc, win, wout, act, dg, dyrows = (R[k] for k in ("rows", "acc", "win", "wout", "act", "dg", "dyrows"))
        dyrows[...] = flat(R["yr"])
        acc[...] = jnp.zeros(acc.shape, F32)

        def ffn(t):
            at = tile(t)
            dact = dot_nt(dyrows[...], wout[at, :])
            dpre = (dact * dg[:, at].astype(F32)).astype(BF16)
            dg[:, at] = dpre
            acc[...] += dot_nt(dpre, win[:, at])
        loop(FF // TILE, ffn)
        R["es"][...] = slots(acc[...])
        spread(R["es"], R["er"], DEXP, l)

        def weights(t):
            at = tile(t)
            win[:, at] = dot_tn(rows[...], dg[:, at]).astype(BF16)
            wout[at, :] = dot_tn(act[:, at], dyrows[...]).astype(BF16)
        loop(FF // TILE, weights)
        pltpu.make_async_copy(win, R["gwin"], rsem.at[OWIN]).start()
        pltpu.make_async_copy(wout, R["gwout"], rsem.at[OWOUT]).start()

        got(R["er"], DEXP)
        dn2 = dot(R["stmat"][...], flat(R["er"]))
        dx, dgain = norm_back(R["hidden"][...], R["gains"][1:2, :], dn2)
        R["sm"][...] = jnp.zeros((8, D), F32)
        R["sm"][1:2, :] = dgain
        dh = g.astype(F32) + dx
        R["dh"][...] = dh
        dattn = dh.astype(BF16)
        dmix = dot_nt(dattn, wo()).astype(BF16)
        dos = R["dos"]
        for u in range(24):
            rs = slice(64 * (u // HEADS), 64 * (u // HEADS) + 64)
            h = 64 * (u % HEADS)
            dos[u, :, 0:64] = dmix[rs, h:h + 64]
        to_heads(dos, R["dor"].at[l], DOUT + l)
        gout = dot_tn(R["mixed"][...], dattn)
        R["gp"][:, :, 2304:3072] = gout.astype(BF16).reshape(16, 48, D)

    def bwd_two(l):
        got(R["dkr"], DQKV + l)
        dkr, dqk, dvv, gp = R["dkr"], R["dqk"], R["dvv"], R["gp"]
        for u in range(24):
            rs = slice(64 * (u // HEADS), 64 * (u // HEADS) + 64)
            h = 64 * (u % HEADS)
            dqk[rs, D + h:D + h + 64] = dkr[u, :, 0:64]
            dvv[rs, h:h + 64] = dkr[u, :, 64:128]
            dqk[rs, h:h + 64] = dkr[u, :, 128:192]
        dn = dot_nt(dqk[...], wk()) + dot_nt(dvv[...], wv())
        dx, dgain = norm_back(layer_in(l).astype(F32), R["gains"][0:1, :], dn)
        low = (R["dh"][...] + dx).astype(BF16)
        R["sgr"][...] = low
        if l == 1:
            R["xsend"][...] = low
            send(R["xsend"], R["gin"], GPASS, 0, s, r)
        R["sm"][0:1, :] = dgain
        nrm = R["nrm"]
        for t in range(6):
            gp[:, :, 256 * t:256 * t + 256] = dot_tn(nrm[...], dqk[:, 256 * t:256 * t + 256]).astype(BF16).reshape(16, 48, 256)
        for t in range(3):
            gp[:, :, 1536 + 256 * t:1792 + 256 * t] = dot_tn(nrm[...], dvv[:, 256 * t:256 * t + 256]).astype(BF16).reshape(16, 48, 256)

        def reduce(i):
            push(gp.at[i], R["gr"].at[s], GW, l, i, r)
            push(R["sm"], R["smr"].at[s], SMALL, l, i, r)
        loop(SHARDS, reduce)

    for l in range(2):
        pl.when(c == l)(lambda l=l: fwd_one(l))
        pl.when(is_head)(lambda l=l: head_fwd(l))
        pl.when(c == l)(lambda l=l: fwd_two(l))
    for l in (1, 0):
        pl.when(c == l)(lambda l=l: bwd_one(l))
        pl.when(is_head)(lambda l=l: head_bwd(l))
        pl.when(c == l)(lambda l=l: bwd_two(l))

    got(R["gr"], GW)
    got(R["smr"], SMALL)
    got(R["gtr"], GTAB)
    gr, gx, sx = R["gr"], R["gx"], R["sx"]
    for t in range(12):
        cols = slice(256 * t, 256 * t + 256)
        part = gr[0, :, cols].astype(F32)
        for k in range(1, SHARDS):
            part = part + gr[k, :, cols].astype(F32)
        R["gxs"][:, cols] = part.astype(BF16)
    small = R["smr"][0]
    for k in range(1, SHARDS):
        small = small + R["smr"][k]
    table = R["gtr"][0]
    for k in range(1, 24):
        table = table + R["gtr"][k]
    R["sxs"][...] = small + jnp.concatenate([table, jnp.zeros((8, D - 128), F32)], axis=1)

    def over_replicas(i):
        push(R["gxs"], gx.at[r], GX, c, s, i)
        push(R["sxs"], sx.at[r], SX, c, s, i)
    loop(REPLICAS, over_replicas)
    got(gx, GX)
    got(sx, SX)
    R["gwo"][...] = (gx[0].astype(F32) + gx[1].astype(F32) + gx[2].astype(F32) + gx[3].astype(F32)).astype(BF16)
    R["smo"][...] = sx[0] + sx[1] + sx[2] + sx[3]

    sent(mr.at[pl.ds(0, 31)], MISC)
    sent(ga.at[0, pl.ds(0, 3)], GA1)
    sent(gb.at[0, pl.ds(0, 3)], GB1)
    sent(ga.at[pl.ds(0, 3)], GA2)
    sent(gb.at[pl.ds(0, 3)], GB2)
    few = EXPERTS - 1
    sent(R["ds"].at[pl.ds(0, few)], DISP)
    sent(R["rs"].at[pl.ds(0, few)], RET)
    sent(R["ys"].at[pl.ds(0, few)], DY)
    sent(R["es"].at[pl.ds(0, few)], DEXP)
    sent(R["gp"].at[pl.ds(0, 15)], GW)
    sent(R["smr"].at[pl.ds(0, 15)], SMALL)
    sent(gx.at[pl.ds(0, 3)], GX)
    sent(sx.at[pl.ds(0, 3)], SX)
    got(R["win"], OWIN)
    got(R["wout"], OWOUT)
    for l in range(2):
        @pl.when(c == l)
        def _():
            sent(R["xsend"], XPASS if l == 0 else GPASS)
            for buf, i in ((R["qs"], QKV + l), (R["dos"], DOUT + l)):
                pl.when(is_head)(lambda buf=buf, i=i: sent(buf.at[pl.ds(0, 23)], i))
                pl.when(jnp.logical_not(is_head))(lambda buf=buf, i=i: sent(buf, i))

        @pl.when(is_head)
        def _():
            for buf, i in ((R["os"], MIX + l), (R["dks"], DQKV + l)):
                pl.when(c == l)(lambda buf=buf, i=i: sent(buf.at[l, pl.ds(0, 15)], i))
                pl.when(c != l)(lambda buf=buf, i=i: sent(buf.at[l], i))

    @pl.when(is_head)
    def _():
        sent(mr.at[pl.ds(0, 31)], GTAB)


def body(tokens, cotangent, wqkv, wout, gain_attn, gain_ffn, rel_table, w_in, w_out_exp, expert_ids, gates, seg_ids, buckets):
    shard = lax.axis_index("shard")
    wcat = jnp.concatenate([wqkv[0], wout[0]], axis=1)
    pad = lambda v, n: jnp.pad(v, ((0, 0), (0, n - v.shape[1])))
    table = rel_table[0].astype(F32).reshape(2, 6, 2).transpose(1, 2, 0)
    table = pad(table.reshape(12, 2), 64).reshape(6, 128)
    misc = jnp.concatenate([pad(gain_attn.astype(F32), 128), pad(gain_ffn.astype(F32), 128), table], axis=0)
    oh = (buckets[::-1][None, :] == jnp.arange(128)[:, None]).astype(BF16)
    oh = pad(oh, BAND)
    seg = lax.dynamic_index_in_dim(seg_ids, lax.axis_index("section"), 0, keepdims=False).astype(F32)
    ids = expert_ids[0].reshape(2, TOK)
    before = (jnp.arange(TOK)[:, None] > jnp.arange(TOK)[None, :])[None]
    rank = jnp.sum(((ids[:, :, None] == ids[:, None, :]) & before).astype(jnp.int32), axis=2)
    slot = (ids * SLOTS + jnp.arange(2)[:, None] * 3 + rank).reshape(TOK, 2)
    gate = gates[0].reshape(TOK, 2)
    every = jnp.arange(SLOT_ROWS)

    def matrices(hit_a, hit_b, gate_a, gate_b):
        full = jnp.where(hit_a, gate_a, 0.0) + jnp.where(hit_b, gate_b, 0.0)
        high = lax.reduce_precision(full, 8, 7)
        return (hit_a | hit_b).astype(BF16), high.astype(BF16), (full - high).astype(BF16)
    smat, gh, gl = matrices(slot[None, :, 0] == every[:, None], slot[None, :, 1] == every[:, None], gate[None, :, 0], gate[None, :, 1])
    stmat, gth, gtl = matrices(slot[:, 0:1] == every[None, :], slot[:, 1:2] == every[None, :], gate[:, 0:1], gate[:, 1:2])

    vmem = pl.BlockSpec(memory_space=pltpu.VMEM)
    hbm = pl.BlockSpec(memory_space=pl.ANY)
    out = jax.ShapeDtypeStruct
    acts, sgr, gwo, smo, gwin, gwout = pl.pallas_call(
        kernel,
        out_shape=(out((TOK, D), BF16), out((TOK, D), BF16), out((48, 3072), BF16), out((8, D), F32), out((D, FF), BF16), out((FF, D), BF16)),
        in_specs=[vmem] * 13 + [hbm] * 2,
        out_specs=(vmem, vmem, vmem, vmem, hbm, hbm),
        scratch_shapes=[pltpu.VMEM(*v) for v in SCRATCH.values()] + [pltpu.SemaphoreType.DMA((32,)), pltpu.SemaphoreType.DMA((32,))],
        compiler_params=pltpu.CompilerParams(has_side_effects=True, vmem_limit_bytes=64 * 1024 * 1024 - 65536),
        name="relay",
    )(tokens.reshape(TOK, D), cotangent.reshape(TOK, D), wcat, misc, oh, seg[None, :], seg[:, None],
      smat, stmat, gh, gl, gth, gtl, w_in[0, 0], w_out_exp[0, 0])
    gains = lax.dynamic_slice(smo, (0, shard * 48), (2, 48)).astype(BF16)
    grad_table = smo[2:8, 0:128].reshape(HEADS, 64)[:, 0:32].T
    grad_table = lax.dynamic_slice(grad_table, (shard * 2, 0), (2, HEADS)).astype(BF16)
    return (
        acts.reshape(1, 2, ROWS, D),
        sgr.reshape(1, 2, ROWS, D),
        gwo[None, :, 0:2304],
        gwo[None, :, 2304:3072],
        gains[0:1],
        gains[1:2],
        grad_table[None],
        gwin[None, None],
        gwout[None, None],
    )


def solution(mesh):
    in_specs = (
        P("replica", "shard", None),
        P("replica", "shard", None),
        P("section", "shard", None),
        P("section", "shard", None),
        P("section", "shard"),
        P("section", "shard"),
        P("section", "shard", None),
        P("section", ("shard", "replica"), None, None),
        P("section", ("shard", "replica"), None, None),
        P("section", "replica", "shard", None),
        P("section", "replica", "shard", None),
        P("replica", None),
        P(),
    )
    out_specs = (
        P("section", "replica", "shard", None),
        P("section", "replica", "shard", None),
        P("section", "shard", None),
        P("section", "shard", None),
        P("section", "shard"),
        P("section", "shard"),
        P("section", "shard", None),
        P("section", ("shard", "replica"), None, None),
        P("section", ("shard", "replica"), None, None),
    )
    return jax.shard_map(body, mesh=mesh, in_specs=in_specs, out_specs=out_specs, check_vma=False)
```

```python
from types import SimpleNamespace

import jax
import jax.numpy as jnp
from jax import lax
from jax.experimental import pallas as pl
from jax.experimental.pallas import tpu as pltpu
from jax.sharding import PartitionSpec as P

MESH = pl.DeviceIdType.MESH
F32 = jnp.float32
BF16 = jnp.bfloat16
HIGH = lax.Precision.HIGHEST

D, HEADS, HD, FF = 768, 12, 64, 3072
LENGTH, ROWS, EXPERTS, SLOTS = 1024, 64, 64, 8
SHARDS, REPLICAS = 16, 4
TOK = 2 * ROWS
SLOT_ROWS = EXPERTS * SLOTS
BAND = LENGTH + 128
TILE = 512
HALF = 1152
C0 = 0.7978845608028654
C1 = C0 * 0.044715

MISC, GA1, GB1, GA2, GB2 = 0, 1, 2, 3, 4
QKV, MIX, DOUT, DQKV = 6, 8, 10, 12
DISP, RET, DY, DEXP, XPASS, GPASS = 14, 15, 16, 17, 18, 19
GTAB, SMALL, GO, GX, SX = 20, 21, 22, 23, 24
WIN, WOUT, OWIN, OWOUT = 25, 26, 27, 28
GW, RA1, RB1, RA2, RB2 = 5, 29, 30, 31, 32

SCRATCH = dict(
    ga=((4, 4, 48, HALF), BF16),
    gb=((4, 4, 48, HALF), BF16),
    gw=((16, 48, D), BF16),
    misc=((8, 128), F32),
    mr=((32, 8, 128), F32),
    gains=((8, D), F32),
    oh=((128, BAND), BF16),
    segr=((1, LENGTH), F32),
    segc=((LENGTH, 1), F32),
    smat=((SLOT_ROWS, TOK), BF16),
    gh=((SLOT_ROWS, TOK), BF16),
    gl=((SLOT_ROWS, TOK), BF16),
    stmat=((TOK, SLOT_ROWS), BF16),
    gth=((TOK, SLOT_ROWS), BF16),
    gtl=((TOK, SLOT_ROWS), BF16),
    tb=((2, 128, LENGTH), F32),
    gg=((128, BAND), F32),
    win=((D, FF), BF16),
    wout=((FF, D), BF16),
    qs=((24, 96, 128), BF16),
    qr=((2, 16, 96, 128), BF16),
    os=((2, 16, 32, 128), BF16),
    mx=((24, 32, 128), BF16),
    mixed=((TOK, D), BF16),
    nrm=((TOK, D), BF16),
    hidden=((TOK, D), F32),
    xsend=((TOK, D), BF16),
    xin=((TOK, D), BF16),
    gin=((TOK, D), BF16),
    ds=((EXPERTS, SLOTS, D), BF16),
    dr=((EXPERTS, SLOTS, D), BF16),
    rs=((EXPERTS, SLOTS, D), BF16),
    rr=((EXPERTS, SLOTS, D), BF16),
    ys=((EXPERTS, SLOTS, D), BF16),
    yr=((EXPERTS, SLOTS, D), BF16),
    es=((EXPERTS, SLOTS, D), BF16),
    er=((EXPERTS, SLOTS, D), BF16),
    rows=((SLOT_ROWS, D), BF16),
    dyrows=((SLOT_ROWS, D), BF16),
    act=((SLOT_ROWS, FF), BF16),
    dg=((SLOT_ROWS, FF), BF16),
    acc=((SLOT_ROWS, D), F32),
    lse=((2, LENGTH, 1), F32),
    dos=((24, 32, 128), BF16),
    dor=((2, 16, 32, 128), BF16),
    dks=((2, 16, 96, 128), BF16),
    dkr=((24, 96, 128), BF16),
    dkv=((LENGTH, 128), F32),
    dqkv=((TOK, 2304), BF16),
    dh=((TOK, D), F32),
    gp=((4, 4, 48, 2304), BF16),
    r1a=((4, 4, 48, HALF), BF16),
    r1b=((4, 4, 48, HALF), BF16),
    p2a=((4, 48, HALF), BF16),
    p2b=((4, 48, HALF), BF16),
    r2a=((4, 48, HALF), BF16),
    r2b=((4, 48, HALF), BF16),
    gop=((16, 48, D), BF16),
    gor=((16, 48, D), BF16),
    gxs=((48, 3072), BF16),
    gx=((4, 48, 3072), BF16),
    sm=((8, D), F32),
    smr=((16, 8, D), F32),
    sxs=((8, D), F32),
    sx=((4, 8, D), F32),
    gts=((2, 8, 128), F32),
    gtr=((24, 8, 128), F32),
)
INPUTS = dict(tok=0, cot=0, wq=0, wo=0, gain1=0, gain2=0, table=0, ids=0, gate=0, seg=0, bk=0, winh=0, wouth=0)
OUTPUTS = dict(acts=0, sgr=0, gqkv=0, gout=0, ggain1=0, ggain2=0, gtable=0, gwin=0, gwout=0)


def dot(a, b, **kw):
    return jnp.dot(a, b, preferred_element_type=F32, **kw)


def dot_nt(a, b, **kw):
    return lax.dot_general(a, b, (((1,), (1,)), ((), ())), preferred_element_type=F32, **kw)


def dot_tn(a, b, **kw):
    return lax.dot_general(a, b, (((0,), (0,)), ((), ())), preferred_element_type=F32, **kw)


def loop(count, step):
    def wrapped(i, carry):
        step(i)
        return carry
    lax.fori_loop(0, count, wrapped, 0)


def kernel(*refs):
    names = tuple(INPUTS) + tuple(OUTPUTS) + tuple(SCRATCH)
    R = SimpleNamespace(**dict(zip(names, refs)))
    ssem, rsem, go = refs[len(names):]
    c = lax.axis_index("section")
    s = lax.axis_index("shard")
    r = lax.axis_index("replica")
    e = s * REPLICAS + r
    y = s // 4
    z = s % 4

    def push(src, dst, i, tc, ts, tr):
        same = (tc == c) & (ts == s) & (tr == r)

        @pl.when(same)
        def _():
            pltpu.make_async_copy(src, dst, rsem.at[i]).start()

        @pl.when(jnp.logical_not(same))
        def _():
            send(src, dst, i, tc, ts, tr)

    def send(src, dst, i, tc, ts, tr):
        pltpu.make_async_remote_copy(
            src_ref=src, dst_ref=dst, send_sem=ssem.at[i], recv_sem=rsem.at[i],
            device_id=(tc, ts, tr), device_id_type=MESH,
        ).start()

    def got(ref, i):
        pltpu.make_async_copy(ref, ref, rsem.at[i]).wait()

    def sent(ref, i):
        pltpu.make_async_copy(ref, ref, ssem.at[i]).wait()

    pltpu.make_async_copy(R.winh, R.win, rsem.at[WIN]).start()
    pltpu.make_async_copy(R.wouth, R.wout, rsem.at[WOUT]).start()

    wq, ga, gb, gw = R.wq, R.ga, R.gb, R.gw

    def gather_one(i):
        push(wq.at[:, pl.ds(0, HALF)], ga.at[y, z], GA1, c, y * 4 + i, r)
        push(wq.at[:, pl.ds(HALF, HALF)], gb.at[y, z], GB1, c, i * 4 + z, r)

    def gather_two(i):
        @pl.when(i != y)
        def _():
            send(ga.at[y], ga.at[y], GA2, c, i * 4 + z, r)

        @pl.when(i != z)
        def _():
            send(gb.at[:, z], gb.at[:, z], GB2, c, y * 4 + i, r)

    def gather_out(i):
        push(R.wo, gw.at[s], GW, c, i, r)

    def gather_start():
        loop(4, gather_one)

    def gather_middle():
        got(ga.at[y], GA1)
        got(gb.at[:, z], GB1)
        loop(4, gather_two)

    def gather_end():
        got(ga.at[pl.ds(0, 3)], GA2)
        got(gb.at[pl.ds(0, 3)], GB2)

    pl.when(c == 0)(gather_start)

    misc = R.misc
    misc[...] = jnp.zeros(misc.shape, F32)
    misc[0:1, 0:48] = R.gain1[...].astype(F32)
    misc[1:2, 0:48] = R.gain2[...].astype(F32)
    table = R.table[...].astype(F32)
    for k in range(2):
        for h in range(HEADS):
            at = (h % 2) * 64 + k
            misc[2 + h // 2:3 + h // 2, at:at + 1] = table[k:k + 1, h:h + 1]

    def misc_step(i):
        push(misc, R.mr.at[c * 16 + s], MISC, i // 16, i % 16, r)
    loop(32, misc_step)

    pl.when(c == 0)(gather_middle)

    r128 = lax.broadcasted_iota(jnp.int32, (TOK, TOK), 0)
    c128 = lax.broadcasted_iota(jnp.int32, (TOK, TOK), 1)
    eye = r128 == c128

    def column(row):
        return jnp.sum(jnp.where(eye, row, 0.0), axis=1, keepdims=True)

    def lay(col):
        return jnp.sum(jnp.where(eye, col, 0.0), axis=0, keepdims=True)
    id_cols = [R.ids[:, k:k + 1].astype(F32) for k in range(2)]
    gate_cols = [R.gate[:, k:k + 1] for k in range(2)]
    id_rows = [lay(v) for v in id_cols]
    gate_rows = [lay(v) for v in gate_cols]
    before = (c128 < r128) & (c128 // ROWS == r128 // ROWS)
    slot_cols = []
    for k in range(2):
        own = id_cols[k]
        same = (own == id_rows[0]).astype(F32) + (own == id_rows[1]).astype(F32)
        rank = jnp.sum(jnp.where(before, same, 0.0), axis=1, keepdims=True)
        part = (lax.broadcasted_iota(jnp.int32, (TOK, 1), 0) // ROWS * 3).astype(F32)
        slot_cols.append(own * SLOTS + part + rank)
    down = lax.broadcasted_iota(jnp.int32, (SLOT_ROWS, TOK), 0).astype(F32)
    across = lax.broadcasted_iota(jnp.int32, (TOK, SLOT_ROWS), 1).astype(F32)

    def matrices(hits, gates, refs):
        full = jnp.where(hits[0], gates[0], 0.0) + jnp.where(hits[1], gates[1], 0.0)
        high = full.astype(BF16)
        refs[0][...] = (hits[0] | hits[1]).astype(F32).astype(BF16)
        refs[1][...] = high
        refs[2][...] = (full - high.astype(F32)).astype(BF16)
    matrices([lay(v) == down for v in slot_cols], gate_rows, (R.smat, R.gh, R.gl))
    matrices([v == across for v in slot_cols], gate_cols, (R.stmat, R.gth, R.gtl))

    seg = R.seg[...].astype(F32)
    R.segr[...] = jnp.where(c == 0, seg[0:1, :], seg[1:2, :])
    for b in range(8):
        R.segc[128 * b:128 * b + 128, :] = column(R.segr[:, 128 * b:128 * b + 128])
    R.oh[...] = jnp.zeros((128, BAND), BF16)
    bk = jnp.broadcast_to(R.bk[...], (8, LENGTH)).astype(F32).astype(BF16)
    turn = (r128 + c128 == 127).astype(F32).astype(BF16)
    bk = jnp.concatenate([dot(bk[:, 896 - 128 * k:1024 - 128 * k], turn) for k in range(8)], axis=1)[0:1, :]
    R.oh[:, 0:LENGTH] = (bk.astype(jnp.int32) == lax.broadcasted_iota(jnp.int32, (128, LENGTH), 0)).astype(F32).astype(BF16)

    got(R.mr, MISC)
    mr = R.mr
    lane = lax.broadcasted_iota(jnp.int32, (8, D), 1)
    total = jnp.zeros((8, D), F32)
    for k in range(SHARDS):
        piece = jnp.concatenate([mr[c * 16 + k], jnp.zeros((8, D - 128), F32)], axis=1)
        piece = jnp.where(lane < 48, piece, 0.0)
        total = total + (pltpu.roll(piece, 48 * k, 1) if k else piece)
    R.gains[...] = total

    is_head = s < HEADS

    @pl.when(is_head)
    def _():
        sub = lax.broadcasted_iota(jnp.int32, (8, 128), 0)
        for l in range(2):
            tab = jnp.zeros((8, 128), F32)
            for k in range(SHARDS):
                tab = tab + (pltpu.roll(mr[l * 16 + k], 2 * k, 1) if k else mr[l * 16 + k])
            tab = jnp.where(sub == 2 + s // 2, tab, 0.0)
            tab = pltpu.roll(tab, (s % 2) * 64, 1)
            row = jnp.sum(tab, axis=0, keepdims=True)
            base = dot(jnp.broadcast_to(row, (8, 128)).astype(BF16), R.oh[...])
            band = jnp.broadcast_to(base[0:1], (128, BAND))
            band = pltpu.roll(band, BAND - 127, 1, stride=1, stride_axis=0)
            R.tb[l] = band[:, :LENGTH]

    @pl.when(c == 0)
    def _():
        gather_end()
        pl.semaphore_signal(go, 1, device_id=(1, s, r), device_id_type=MESH)

    @pl.when(c == 1)
    def _():
        pl.semaphore_wait(go, 1)
        gather_start()
        gather_middle()
    loop(SHARDS, gather_out)

    def unpack(part):
        return jnp.concatenate([part[:, :, 0:64], part[:, :, 64:128]], axis=1).reshape(part.shape[0] * 64, 64)

    def pack(value):
        value = value.astype(BF16).reshape(2, 64, 64)
        return jnp.concatenate([value[:, 0:32], value[:, 32:64]], axis=2)

    def head_parts(l):
        both = R.qr[l, :, 0:64, :].reshape(LENGTH, 128)
        q = unpack(R.qr[l, :, 64:96, :])
        return both[:, 0:64], both[:, 64:128], q * BF16(0.125)

    def logits(l, b, q, keys):
        nk = 128 * (b + 1)
        scores = dot_nt(q[128 * b:nk], keys[:nk]) + R.tb[l, :, 896 - 128 * b:1024]
        row = lax.broadcasted_iota(jnp.int32, (128, nk), 0) + 128 * b
        col = lax.broadcasted_iota(jnp.int32, (128, nk), 1)
        ok = (col <= row) & (R.segc[128 * b:nk, :] == R.segr[:, :nk])
        return jnp.where(ok, scores, -1e30)

    def head_fwd(l):
        got(R.qr.at[l], QKV + l)
        keys, values, q = head_parts(l)
        for b in range(8):
            nk = 128 * (b + 1)
            lg = logits(l, b, q, keys)
            top = jnp.max(lg, axis=1, keepdims=True)
            ex = jnp.exp(lg - top)
            tot = jnp.sum(ex, axis=1, keepdims=True)
            out = dot(ex.astype(BF16), values[:nk]) / tot
            R.os[l, 2 * b:2 * b + 2] = pack(out)
            R.lse[l, 128 * b:nk, :] = top + jnp.log(tot)

        def back(i):
            push(R.os.at[l, i], R.mx.at[c * HEADS + s], MIX + l, l, i, r)
        loop(SHARDS, back)

    def head_bwd(l):
        got(R.dor.at[l], DOUT + l)
        keys, values, q = head_parts(l)
        dor, dks, dkv, gg = R.dor, R.dks, R.dkv, R.gg
        dkv[...] = jnp.zeros(dkv.shape, F32)
        gg[...] = jnp.zeros(gg.shape, F32)
        for b in range(8):
            nk = 128 * (b + 1)
            qb = q[128 * b:nk]
            prob = jnp.exp(logits(l, b, q, keys) - R.lse[l, 128 * b:nk, :])
            do = unpack(dor[l, 2 * b:2 * b + 2])
            dp = dot_nt(do, values[:nk])
            delta = jnp.sum(prob * dp, axis=1, keepdims=True)
            dlog = prob * (dp - delta)
            gg[:, 896 - 128 * b:1024] += dlog
            low = dlog.astype(BF16)
            dq = dot(low, keys[:nk]) * 0.125
            dks[l, 2 * b:2 * b + 2, 64:96, :] = pack(dq)
            dkv[:nk, 0:64] += dot_tn(low, qb)
            dkv[:nk, 64:128] += dot_tn(prob.astype(BF16), do)
        dks[l, :, 0:64, :] = dkv[...].astype(BF16).reshape(16, 64, 128)

        def back(i):
            push(dks.at[l, i], R.dkr.at[c * HEADS + s], DQKV + l, l, i, r)
        loop(SHARDS, back)
        flip = (lax.broadcasted_iota(jnp.int32, (128, 128), 0) + lax.broadcasted_iota(jnp.int32, (128, 128), 1)) == 127
        band = dot(flip.astype(F32), gg[...], precision=HIGH)
        band = pltpu.roll(band, 0, 1, stride=1, stride_axis=0)
        diag = jnp.sum(band, axis=0, keepdims=True)
        tg = dot_nt(jnp.broadcast_to(diag, (8, BAND)), R.oh[...].astype(F32), precision=HIGH)
        sub = lax.broadcasted_iota(jnp.int32, (8, 128), 0)
        tg = jnp.where(sub == 2 + s // 2, pltpu.roll(tg, (s % 2) * 64, 1), 0.0)
        R.gts[l] = tg

        def back_table(i):
            push(R.gts.at[l], R.gtr.at[c * HEADS + s], GTAB, l, i, r)
        loop(SHARDS, back_table)

    def norm(x):
        return x * lax.rsqrt(jnp.mean(x * x, axis=1, keepdims=True) + 1e-06)

    def norm_back(x, gain, dn):
        rstd = lax.rsqrt(jnp.mean(x * x, axis=1, keepdims=True) + 1e-06)
        n = x * rstd
        dgain = jnp.sum(dn * n, axis=0, keepdims=True)
        dng = dn * gain
        return rstd * (dng - n * jnp.mean(dng * n, axis=1, keepdims=True)), dgain

    def spread(buf, dst, i, l):
        def step(k):
            push(buf.at[k], dst.at[e], i, l, k // REPLICAS, k % REPLICAS)
        loop(EXPERTS, step)

    def slots(value):
        return value.reshape(EXPERTS, SLOTS, D).astype(BF16)

    def flat(ref):
        return ref[...].astype(F32).reshape(SLOT_ROWS, D).astype(BF16)

    def to_heads(buf, dst, i):
        def step(u):
            push(buf.at[u], dst.at[s], i, u // HEADS, u % HEADS, r)
        loop(24, step)

    def tile(t):
        return pl.ds(pl.multiple_of(t * TILE, TILE), TILE)

    def layer_in(l):
        return R.tok[...] if l == 0 else R.xin[...]

    def wa():
        return ga[...].reshape(D, HALF)

    def wb():
        return gb[...].reshape(D, HALF)

    def wo():
        return gw[...].reshape(D, D)

    def fwd_one(l):
        if l == 1:
            got(R.xin, XPASS)
            gather_end()
        x = layer_in(l).astype(F32)
        nrm = (norm(x) * R.gains[0:1, :]).astype(BF16)
        R.nrm[...] = nrm
        qkv = jnp.concatenate([dot(nrm, wa()).astype(BF16), dot(nrm, wb()).astype(BF16)], axis=1)
        qs = R.qs
        for u in range(24):
            at = 64 * (u // HEADS)
            h = 64 * (u % HEADS)
            qs[u, 0:64, 0:64] = qkv[at:at + 64, D + h:D + h + 64]
            qs[u, 0:64, 64:128] = qkv[at:at + 64, 2 * D + h:2 * D + h + 64]
            qs[u, 64:96, 0:64] = qkv[at:at + 32, h:h + 64]
            qs[u, 64:96, 64:128] = qkv[at + 32:at + 64, h:h + 64]
        to_heads(qs, R.qr.at[l], QKV + l)

    def fwd_two(l):
        got(R.mx, MIX + l)
        mx, mixed = R.mx, R.mixed
        for u in range(24):
            at = 64 * (u // HEADS)
            h = 64 * (u % HEADS)
            mixed[at:at + 32, h:h + 64] = mx[u, :, 0:64]
            mixed[at + 32:at + 64, h:h + 64] = mx[u, :, 64:128]
        got(gw, GW)
        hidden = layer_in(l).astype(F32) + dot(mixed[...], wo())
        R.hidden[...] = hidden
        nrm2 = (norm(hidden) * R.gains[1:2, :]).astype(BF16)
        R.ds[...] = slots(dot(R.smat[...], nrm2))
        spread(R.ds, R.dr, DISP, l)

        got(R.win, WIN)
        got(R.wout, WOUT)
        got(R.dr, DISP)
        rows, acc, win, wout = R.rows, R.acc, R.win, R.wout
        rows[...] = flat(R.dr)
        acc[...] = jnp.zeros(acc.shape, F32)

        def ffn(t):
            at = tile(t)
            pre = dot(rows[...], win[:, at])
            sq = pre * pre
            half = 0.5 + 0.5 * jnp.tanh(pre * (C0 + C1 * sq))
            act = (pre * half).astype(BF16)
            R.act[:, at] = act
            R.dg[:, at] = (half + pre * (half * (1.0 - half)) * (2.0 * C0 + 6.0 * C1 * sq)).astype(BF16)
            acc[...] += dot(act, wout[at, :])
        loop(FF // TILE, ffn)
        R.rs[...] = slots(acc[...])
        spread(R.rs, R.rr, RET, l)
        got(R.rr, RET)
        back = flat(R.rr)
        out = R.hidden[...] + dot(R.gth[...], back) + dot(R.gtl[...], back)
        R.acts[...] = out.astype(BF16)
        if l == 0:
            R.xsend[...] = out.astype(BF16)
            send(R.xsend, R.xin, XPASS, 1, s, r)

    def bwd_one(l):
        if l == 0:
            got(R.gin, GPASS)
        g = R.cot[...] if l == 1 else R.gin[...]
        R.ys[...] = slots(dot(R.gh[...], g) + dot(R.gl[...], g))
        spread(R.ys, R.yr, DY, l)
        got(R.yr, DY)
        rows, acc, win, wout, act, dg, dyrows = (R.rows, R.acc, R.win, R.wout, R.act, R.dg, R.dyrows)
        dyrows[...] = flat(R.yr)
        acc[...] = jnp.zeros(acc.shape, F32)

        def ffn(t):
            at = tile(t)
            dact = dot_nt(dyrows[...], wout[at, :])
            dpre = (dact * dg[:, at].astype(F32)).astype(BF16)
            dg[:, at] = dpre
            acc[...] += dot_nt(dpre, win[:, at])
        loop(FF // TILE, ffn)
        R.es[...] = slots(acc[...])
        spread(R.es, R.er, DEXP, l)

        def weights(t):
            at = tile(t)
            win[:, at] = dot_tn(rows[...], dg[:, at]).astype(BF16)
            wout[at, :] = dot_tn(act[:, at], dyrows[...]).astype(BF16)
        loop(FF // TILE, weights)
        pltpu.make_async_copy(win, R.gwin, rsem.at[OWIN]).start()
        pltpu.make_async_copy(wout, R.gwout, rsem.at[OWOUT]).start()

        got(R.er, DEXP)
        dn2 = dot(R.stmat[...], flat(R.er))
        dx, dgain = norm_back(R.hidden[...], R.gains[1:2, :], dn2)
        R.sm[...] = jnp.zeros((8, D), F32)
        R.sm[1:2, :] = dgain
        dh = g.astype(F32) + dx
        R.dh[...] = dh
        dattn = dh.astype(BF16)
        dmix = dot_nt(dattn, wo()).astype(BF16)
        dos = R.dos
        for u in range(24):
            at = 64 * (u // HEADS)
            h = 64 * (u % HEADS)
            dos[u, :, 0:64] = dmix[at:at + 32, h:h + 64]
            dos[u, :, 64:128] = dmix[at + 32:at + 64, h:h + 64]
        to_heads(dos, R.dor.at[l], DOUT + l)
        gout = dot_tn(R.mixed[...], dattn)
        R.gop[...] = gout.astype(BF16).reshape(16, 48, D)

        def reduce_out(i):
            push(R.gop.at[i], R.gor.at[s], GO, l, i, r)
        loop(SHARDS, reduce_out)

    def bwd_two(l):
        got(R.dkr, DQKV + l)
        dkr, dqkv, gp = R.dkr, R.dqkv, R.gp
        for u in range(24):
            at = 64 * (u // HEADS)
            h = 64 * (u % HEADS)
            dqkv[at:at + 64, D + h:D + h + 64] = dkr[u, 0:64, 0:64]
            dqkv[at:at + 64, 2 * D + h:2 * D + h + 64] = dkr[u, 0:64, 64:128]
            dqkv[at:at + 32, h:h + 64] = dkr[u, 64:96, 0:64]
            dqkv[at + 32:at + 64, h:h + 64] = dkr[u, 64:96, 64:128]
        nrm = R.nrm
        for t in range(9):
            at = slice(256 * t, 256 * t + 256)
            gp[:, :, :, at] = dot_tn(nrm[...], dqkv[:, at]).astype(BF16).reshape(4, 4, 48, 256)

        def reduce_one(i):
            push(gp.at[:, i, :, pl.ds(0, HALF)], R.r1a.at[z], RA1, l, y * 4 + i, r)
            push(gp.at[i, :, :, pl.ds(HALF, HALF)], R.r1b.at[y], RB1, l, i * 4 + z, r)
        loop(4, reduce_one)
        dn = dot_nt(dqkv[:, 0:HALF], wa()) + dot_nt(dqkv[:, HALF:2 * HALF], wb())
        dx, dgain = norm_back(layer_in(l).astype(F32), R.gains[0:1, :], dn)
        low = (R.dh[...] + dx).astype(BF16)
        R.sgr[...] = low
        if l == 1:
            R.xsend[...] = low
            send(R.xsend, R.gin, GPASS, 0, s, r)
        R.sm[0:1, :] = dgain

        def reduce_small(i):
            push(R.sm, R.smr.at[s], SMALL, l, i, r)
        loop(SHARDS, reduce_small)

    def reduce(l):
        r1a, r1b, r2a, r2b, gx, sx = (R.r1a, R.r1b, R.r2a, R.r2b, R.gx, R.sx)

        def four(ref, at):
            return ref[(0,) + at].astype(F32) + ref[(1,) + at].astype(F32) + ref[(2,) + at].astype(F32) + ref[(3,) + at].astype(F32)

        got(r1a, RA1)
        got(r1b, RB1)
        for k in range(4):
            R.p2a[k] = four(r1a, (k,)).astype(BF16)
            R.p2b[k] = four(r1b, (k,)).astype(BF16)

        def reduce_two(i):
            push(R.p2a.at[i], r2a.at[y], RA2, l, i * 4 + z, r)
            push(R.p2b.at[i], r2b.at[z], RB2, l, y * 4 + i, r)
        loop(4, reduce_two)

        got(R.gor, GO)
        part = R.gor[0].astype(F32)
        for k in range(1, SHARDS):
            part = part + R.gor[k].astype(F32)
        R.gxs[:, 2304:3072] = part.astype(BF16)
        got(R.smr, SMALL)
        got(R.gtr, GTAB)
        small = R.smr[0]
        for k in range(1, SHARDS):
            small = small + R.smr[k]
        table = R.gtr[0]
        for k in range(1, 24):
            table = table + R.gtr[k]
        R.sxs[...] = small + jnp.concatenate([table, jnp.zeros((8, D - 128), F32)], axis=1)
        got(r2a, RA2)
        got(r2b, RB2)
        R.gxs[:, 0:HALF] = four(r2a, ()).astype(BF16)
        R.gxs[:, HALF:2 * HALF] = four(r2b, ()).astype(BF16)

        def over_replicas(i):
            push(R.gxs, gx.at[r], GX, c, s, i)
            push(R.sxs, sx.at[r], SX, c, s, i)
        loop(REPLICAS, over_replicas)
        got(gx, GX)
        got(sx, SX)
        grads = four(gx, ()).astype(BF16)
        R.gqkv[...] = grads[:, 0:2304]
        R.gout[...] = grads[:, 2304:3072]
        total = four(sx, ())
        mine = pltpu.roll(total, lax.rem(D - 48 * s, D), 1)
        R.ggain1[...] = mine[0:1, 0:48].astype(BF16)
        R.ggain2[...] = mine[1:2, 0:48].astype(BF16)
        rows = pltpu.roll(total[:, 0:128], lax.rem(128 - 2 * s, 128), 1)
        sent(mr.at[pl.ds(0, 31)], MISC)
        spare = R.misc
        for k in range(2):
            for h in range(HEADS):
                at = (h % 2) * 64 + k
                spare[k:k + 1, h:h + 1] = rows[2 + h // 2:3 + h // 2, at:at + 1]
        R.gtable[...] = spare[0:2, 0:HEADS].astype(BF16)

    for l in range(2):
        pl.when(c == l)(lambda l=l: fwd_one(l))
        pl.when(is_head)(lambda l=l: head_fwd(l))
        pl.when(c == l)(lambda l=l: fwd_two(l))
    for l in (1, 0):
        pl.when(c == l)(lambda l=l: bwd_one(l))
        pl.when(is_head)(lambda l=l: head_bwd(l))
        pl.when(c == l)(lambda l=l: bwd_two(l))
        pl.when(c == l)(lambda l=l: reduce(l))

    sent(ga.at[0, pl.ds(0, 3)], GA1)
    sent(gb.at[0, pl.ds(0, 3)], GB1)
    sent(ga.at[pl.ds(0, 3)], GA2)
    sent(gb.at[pl.ds(0, 3)], GB2)
    few = EXPERTS - 1
    sent(R.ds.at[pl.ds(0, few)], DISP)
    sent(R.rs.at[pl.ds(0, few)], RET)
    sent(R.ys.at[pl.ds(0, few)], DY)
    sent(R.es.at[pl.ds(0, few)], DEXP)
    sent(gw.at[pl.ds(0, 15)], GW)
    sent(R.gop.at[pl.ds(0, 15)], GO)
    sent(R.r1a.at[pl.ds(0, 3)], RA1)
    sent(R.r1b.at[pl.ds(0, 3)], RB1)
    sent(R.p2a.at[pl.ds(0, 3)], RA2)
    sent(R.p2b.at[pl.ds(0, 3)], RB2)
    sent(R.smr.at[pl.ds(0, 15)], SMALL)
    sent(R.gx.at[pl.ds(0, 3)], GX)
    sent(R.sx.at[pl.ds(0, 3)], SX)
    got(R.win, OWIN)
    got(R.wout, OWOUT)
    for l in range(2):
        @pl.when(c == l)
        def _():
            sent(R.xsend, XPASS if l == 0 else GPASS)
            for buf, i in ((R.qs, QKV + l), (R.dos, DOUT + l)):
                pl.when(is_head)(lambda buf=buf, i=i: sent(buf.at[pl.ds(0, 23)], i))
                pl.when(jnp.logical_not(is_head))(lambda buf=buf, i=i: sent(buf, i))

        @pl.when(is_head)
        def _():
            for buf, i in ((R.os, MIX + l), (R.dks, DQKV + l)):
                pl.when(c == l)(lambda buf=buf, i=i: sent(buf.at[l, pl.ds(0, 15)], i))
                pl.when(c != l)(lambda buf=buf, i=i: sent(buf.at[l], i))

    @pl.when(is_head)
    def _():
        sent(mr.at[pl.ds(0, 31)], GTAB)


def settle(*refs):
    ins, outs, held, sems = refs[:9], refs[9:18], refs[18:27], refs[27]
    pieces = [(i, pl.ds(0, ins[i].shape[0])) for i in range(7)]
    for i in (7, 8):
        step = ins[i].shape[0] // 6
        pieces += [(i, pl.ds(k * step, step)) for k in range(6)]
    into = [pltpu.make_async_copy(ins[i].at[at], held[i].at[at], sems.at[0, n]) for n, (i, at) in enumerate(pieces)]
    out = [pltpu.make_async_copy(held[i].at[at], outs[i].at[at], sems.at[1, n]) for n, (i, at) in enumerate(pieces)]
    for copy in into:
        copy.start()
    for first, second in zip(into, out):
        first.wait()
        second.start()
    for copy in out:
        copy.wait()


def body(tokens, cotangent, wqkv, wout, gain_attn, gain_ffn, rel_table, w_in, w_out_exp, expert_ids, gates, seg_ids, buckets):
    vmem = pl.BlockSpec(memory_space=pltpu.VMEM)
    hbm = pl.BlockSpec(memory_space=pl.ANY)
    shapes = ((TOK, D), (TOK, D), (48, 2304), (48, D), (1, 48), (1, 48), (2, HEADS), (D, FF), (FF, D))
    shapes = tuple(jax.ShapeDtypeStruct(v, BF16) for v in shapes)
    scratch = [pltpu.VMEM(*v) for v in SCRATCH.values()]
    outs = pl.pallas_call(
        kernel,
        out_shape=shapes,
        in_specs=[vmem] * 11 + [hbm] * 2,
        out_specs=(vmem,) * 7 + (hbm, hbm),
        scratch_shapes=scratch + [pltpu.SemaphoreType.DMA((33,)), pltpu.SemaphoreType.DMA((33,)), pltpu.SemaphoreType.REGULAR],
        compiler_params=pltpu.CompilerParams(has_side_effects=True, vmem_limit_bytes=64 * 1024 * 1024 - 65536),
        name="relay",
    )(tokens.reshape(TOK, D), cotangent.reshape(TOK, D), wqkv[0], wout[0], gain_attn, gain_ffn, rel_table[0],
      expert_ids.reshape(TOK, 2), gates.reshape(TOK, 2), seg_ids, buckets[None, :], w_in[0, 0], w_out_exp[0, 0])
    outs = pl.pallas_call(
        settle,
        out_shape=shapes,
        in_specs=[hbm] * 9,
        out_specs=(hbm,) * 9,
        scratch_shapes=[pltpu.VMEM(v.shape, BF16) for v in shapes] + [pltpu.SemaphoreType.DMA((2, 19))],
        compiler_params=pltpu.CompilerParams(vmem_limit_bytes=56 * 1024 * 1024),
        name="settle",
    )(*outs)
    acts, sgr, gqkv, gout, ggain1, ggain2, gtable, gwin, gwout = outs
    return (
        acts.reshape(1, 2, ROWS, D),
        sgr.reshape(1, 2, ROWS, D),
        gqkv[None],
        gout[None],
        ggain1,
        ggain2,
        gtable[None],
        gwin[None, None],
        gwout[None, None],
    )


def solution(mesh):
    in_specs = (
        P("replica", "shard", None),
        P("replica", "shard", None),
        P("section", "shard", None),
        P("section", "shard", None),
        P("section", "shard"),
        P("section", "shard"),
        P("section", "shard", None),
        P("section", ("shard", "replica"), None, None),
        P("section", ("shard", "replica"), None, None),
        P("section", "replica", "shard", None),
        P("section", "replica", "shard", None),
        P("replica", None),
        P(),
    )
    out_specs = (
        P("section", "replica", "shard", None),
        P("section", "replica", "shard", None),
        P("section", "shard", None),
        P("section", "shard", None),
        P("section", "shard"),
        P("section", "shard"),
        P("section", "shard", None),
        P("section", ("shard", "replica"), None, None),
        P("section", ("shard", "replica"), None, None),
    )
    return jax.shard_map(body, mesh=mesh, in_specs=in_specs, out_specs=out_specs, check_vma=False)
```

```python
from types import SimpleNamespace

import jax
import jax.numpy as jnp
from jax import lax
from jax.experimental import pallas as pl
from jax.experimental.pallas import tpu as pltpu
from jax.sharding import PartitionSpec as P

MESH = pl.DeviceIdType.MESH
F32 = jnp.float32
BF16 = jnp.bfloat16
HIGH = lax.Precision.HIGHEST

D, HEADS, HD, FF = 768, 12, 64, 3072
LENGTH, ROWS, EXPERTS, SLOTS = 1024, 64, 64, 8
SHARDS, REPLICAS = 16, 4
TOK = 2 * ROWS
SLOT_ROWS = EXPERTS * SLOTS
BAND = LENGTH + 128
TILE = 512
HALF = 1152
C0 = 0.7978845608028654
C1 = C0 * 0.044715

MISC, GA1, GB1, GA2, GB2 = 0, 1, 2, 3, 4
QKV, MIX, DOUT, DQKV = 6, 8, 10, 12
DISP, RET, DY, DEXP, XPASS, GPASS = 14, 15, 16, 17, 18, 19
GTAB, SMALL, GO, GX, SX = 20, 21, 22, 23, 24
WIN, WOUT, OWIN, OWOUT = 25, 26, 27, 28
GW, RA1, RB1, RA2, RB2 = 5, 29, 30, 31, 32

SCRATCH = dict(
    ga=((4, 4, 48, HALF), BF16),
    gb=((4, 4, 48, HALF), BF16),
    gw=((16, 48, D), BF16),
    misc=((8, 128), F32),
    mr=((32, 8, 128), F32),
    gains=((8, D), F32),
    oh=((128, BAND), BF16),
    segr=((1, LENGTH), F32),
    segc=((LENGTH, 1), F32),
    smat=((SLOT_ROWS, TOK), BF16),
    gh=((SLOT_ROWS, TOK), BF16),
    gl=((SLOT_ROWS, TOK), BF16),
    stmat=((TOK, SLOT_ROWS), BF16),
    gth=((TOK, SLOT_ROWS), BF16),
    gtl=((TOK, SLOT_ROWS), BF16),
    tb=((2, 128, LENGTH), F32),
    gg=((128, BAND), F32),
    win=((D, FF), BF16),
    wout=((FF, D), BF16),
    qs=((24, 96, 128), BF16),
    qr=((2, 16, 96, 128), BF16),
    os=((2, 16, 32, 128), BF16),
    mx=((24, 32, 128), BF16),
    mixed=((TOK, D), BF16),
    nrm=((TOK, D), BF16),
    hidden=((TOK, D), F32),
    xsend=((TOK, D), BF16),
    xin=((TOK, D), BF16),
    gin=((TOK, D), BF16),
    ds=((EXPERTS, SLOTS, D), BF16),
    dr=((EXPERTS, SLOTS, D), BF16),
    rs=((EXPERTS, SLOTS, D), BF16),
    rr=((EXPERTS, SLOTS, D), BF16),
    ys=((EXPERTS, SLOTS, D), BF16),
    yr=((EXPERTS, SLOTS, D), BF16),
    es=((EXPERTS, SLOTS, D), BF16),
    er=((EXPERTS, SLOTS, D), BF16),
    rows=((SLOT_ROWS, D), BF16),
    dyrows=((SLOT_ROWS, D), BF16),
    act=((SLOT_ROWS, FF), BF16),
    dg=((SLOT_ROWS, FF), BF16),
    lse=((2, LENGTH, 1), F32),
    dos=((24, 32, 128), BF16),
    dor=((2, 16, 32, 128), BF16),
    dks=((2, 16, 96, 128), BF16),
    dkr=((24, 96, 128), BF16),
    dkv=((LENGTH, 128), F32),
    dqkv=((TOK, 2304), BF16),
    dh=((TOK, D), F32),
    gp=((4, 4, 48, 2304), BF16),
    r1a=((4, 4, 48, HALF), BF16),
    r1b=((4, 4, 48, HALF), BF16),
    p2a=((4, 48, HALF), BF16),
    p2b=((4, 48, HALF), BF16),
    r2a=((4, 48, HALF), BF16),
    r2b=((4, 48, HALF), BF16),
    gop=((16, 48, D), BF16),
    gor=((16, 48, D), BF16),
    gxs=((48, 3072), BF16),
    gx=((4, 48, 3072), BF16),
    sm=((8, D), F32),
    smr=((16, 8, D), F32),
    sxs=((8, D), F32),
    sx=((4, 8, D), F32),
    gts=((2, 8, 128), F32),
    gtr=((24, 8, 128), F32),
)
INPUTS = dict(tok=0, cot=0, wq=0, wo=0, gain1=0, gain2=0, table=0, ids=0, gate=0, seg=0, bk=0, winh=0, wouth=0)
OUTPUTS = dict(acts=0, sgr=0, gqkv=0, gout=0, ggain1=0, ggain2=0, gtable=0, gwin=0, gwout=0)


def dot(a, b, **kw):
    return jnp.dot(a, b, preferred_element_type=F32, **kw)


def dot_nt(a, b, **kw):
    return lax.dot_general(a, b, (((1,), (1,)), ((), ())), preferred_element_type=F32, **kw)


def dot_tn(a, b, **kw):
    return lax.dot_general(a, b, (((0,), (0,)), ((), ())), preferred_element_type=F32, **kw)


def loop(count, step):
    def wrapped(i, carry):
        step(i)
        return carry
    lax.fori_loop(0, count, wrapped, 0)


def kernel(*refs):
    names = tuple(INPUTS) + tuple(OUTPUTS) + tuple(SCRATCH)
    R = SimpleNamespace(**dict(zip(names, refs)))
    ssem, rsem, go = refs[len(names):]
    c = lax.axis_index("section")
    s = lax.axis_index("shard")
    r = lax.axis_index("replica")
    e = s * REPLICAS + r
    y = s // 4
    z = s % 4

    def push(src, dst, i, tc, ts, tr):
        same = (tc == c) & (ts == s) & (tr == r)

        @pl.when(same)
        def _():
            pltpu.make_async_copy(src, dst, rsem.at[i]).start()

        @pl.when(jnp.logical_not(same))
        def _():
            send(src, dst, i, tc, ts, tr)

    def send(src, dst, i, tc, ts, tr):
        pltpu.make_async_remote_copy(
            src_ref=src, dst_ref=dst, send_sem=ssem.at[i], recv_sem=rsem.at[i],
            device_id=(tc, ts, tr), device_id_type=MESH,
        ).start()

    def got(ref, i):
        pltpu.make_async_copy(ref, ref, rsem.at[i]).wait()

    def sent(ref, i):
        pltpu.make_async_copy(ref, ref, ssem.at[i]).wait()

    pltpu.make_async_copy(R.winh, R.win, rsem.at[WIN]).start()
    pltpu.make_async_copy(R.wouth, R.wout, rsem.at[WOUT]).start()

    wq, ga, gb, gw = R.wq, R.ga, R.gb, R.gw

    def gather_one(i):
        push(wq.at[:, pl.ds(0, HALF)], ga.at[y, z], GA1, c, y * 4 + i, r)
        push(wq.at[:, pl.ds(HALF, HALF)], gb.at[y, z], GB1, c, i * 4 + z, r)

    def gather_two(i):
        @pl.when(i != y)
        def _():
            send(ga.at[y], ga.at[y], GA2, c, i * 4 + z, r)

        @pl.when(i != z)
        def _():
            send(gb.at[:, z], gb.at[:, z], GB2, c, y * 4 + i, r)

    def gather_out(i):
        push(R.wo, gw.at[s], GW, c, i, r)

    def gather_start():
        loop(4, gather_one)

    def gather_middle():
        got(ga.at[y], GA1)
        got(gb.at[:, z], GB1)
        loop(4, gather_two)

    def gather_end():
        got(ga.at[pl.ds(0, 3)], GA2)
        got(gb.at[pl.ds(0, 3)], GB2)

    pl.when(c == 0)(gather_start)

    misc = R.misc
    misc[...] = jnp.zeros(misc.shape, F32)
    misc[0:1, 0:48] = R.gain1[...].astype(F32)
    misc[1:2, 0:48] = R.gain2[...].astype(F32)
    table = R.table[...].astype(F32)
    for k in range(2):
        for h in range(HEADS):
            at = (h % 2) * 64 + k
            misc[2 + h // 2:3 + h // 2, at:at + 1] = table[k:k + 1, h:h + 1]

    def misc_step(i):
        push(misc, R.mr.at[c * 16 + s], MISC, i // 16, i % 16, r)
    loop(32, misc_step)

    pl.when(c == 0)(gather_middle)

    r128 = lax.broadcasted_iota(jnp.int32, (TOK, TOK), 0)
    c128 = lax.broadcasted_iota(jnp.int32, (TOK, TOK), 1)
    eye = r128 == c128

    def column(row):
        return jnp.sum(jnp.where(eye, row, 0.0), axis=1, keepdims=True)

    def lay(col):
        return jnp.sum(jnp.where(eye, col, 0.0), axis=0, keepdims=True)
    got(R.mr, MISC)
    mr = R.mr
    lane = lax.broadcasted_iota(jnp.int32, (8, D), 1)
    total = jnp.zeros((8, D), F32)
    for k in range(SHARDS):
        piece = jnp.concatenate([mr[c * 16 + k], jnp.zeros((8, D - 128), F32)], axis=1)
        piece = jnp.where(lane < 48, piece, 0.0)
        total = total + (pltpu.roll(piece, 48 * k, 1) if k else piece)
    R.gains[...] = total

    is_head = s < HEADS

    def set_routes():
        id_cols = [R.ids[:, k:k + 1].astype(F32) for k in range(2)]
        gate_cols = [R.gate[:, k:k + 1] for k in range(2)]
        id_rows = [lay(v) for v in id_cols]
        gate_rows = [lay(v) for v in gate_cols]
        before = (c128 < r128) & (c128 // ROWS == r128 // ROWS)
        slot_cols = []
        for k in range(2):
            own = id_cols[k]
            same = (own == id_rows[0]).astype(F32) + (own == id_rows[1]).astype(F32)
            rank = jnp.sum(jnp.where(before, same, 0.0), axis=1, keepdims=True)
            part = (lax.broadcasted_iota(jnp.int32, (TOK, 1), 0) // ROWS * 3).astype(F32)
            slot_cols.append(own * SLOTS + part + rank)
        down = lax.broadcasted_iota(jnp.int32, (SLOT_ROWS, TOK), 0).astype(F32)
        across = lax.broadcasted_iota(jnp.int32, (TOK, SLOT_ROWS), 1).astype(F32)

        def matrices(hits, gates, refs):
            full = jnp.where(hits[0], gates[0], 0.0) + jnp.where(hits[1], gates[1], 0.0)
            high = full.astype(BF16)
            refs[0][...] = (hits[0] | hits[1]).astype(F32).astype(BF16)
            refs[1][...] = high
            refs[2][...] = (full - high.astype(F32)).astype(BF16)
        matrices([lay(v) == down for v in slot_cols], gate_rows, (R.smat, R.gh, R.gl))
        matrices([v == across for v in slot_cols], gate_cols, (R.stmat, R.gth, R.gtl))

    def set_heads():
        seg = R.seg[...].astype(F32)
        R.segr[...] = jnp.where(c == 0, seg[0:1, :], seg[1:2, :])
        for b in range(8):
            R.segc[128 * b:128 * b + 128, :] = column(R.segr[:, 128 * b:128 * b + 128])
        R.oh[...] = jnp.zeros((128, BAND), BF16)
        bk = jnp.broadcast_to(R.bk[...], (8, LENGTH)).astype(F32).astype(BF16)
        turn = (r128 + c128 == 127).astype(F32).astype(BF16)
        bk = jnp.concatenate([dot(bk[:, 896 - 128 * k:1024 - 128 * k], turn) for k in range(8)], axis=1)[0:1, :]
        R.oh[:, 0:LENGTH] = (bk.astype(jnp.int32) == lax.broadcasted_iota(jnp.int32, (128, LENGTH), 0)).astype(F32).astype(BF16)

        sub = lax.broadcasted_iota(jnp.int32, (8, 128), 0)
        for l in range(2):
            tab = jnp.zeros((8, 128), F32)
            for k in range(SHARDS):
                tab = tab + (pltpu.roll(mr[l * 16 + k], 2 * k, 1) if k else mr[l * 16 + k])
            tab = jnp.where(sub == 2 + s // 2, tab, 0.0)
            tab = pltpu.roll(tab, (s % 2) * 64, 1)
            row = jnp.sum(tab, axis=0, keepdims=True)
            base = dot(jnp.broadcast_to(row, (8, 128)).astype(BF16), R.oh[...])
            band = jnp.broadcast_to(base[0:1], (128, BAND))
            band = pltpu.roll(band, BAND - 127, 1, stride=1, stride_axis=0)
            R.tb[l] = band[:, :LENGTH]

    @pl.when(c == 0)
    def _():
        gather_end()
        pl.semaphore_signal(go, 1, device_id=(1, s, r), device_id_type=MESH)

    pl.when((c == 1) & is_head)(set_heads)

    @pl.when(c == 1)
    def _():
        pl.semaphore_wait(go, 1)
        gather_start()
        gather_middle()
    loop(SHARDS, gather_out)

    def unpack(part):
        return jnp.concatenate([part[:, :, 0:64], part[:, :, 64:128]], axis=1).reshape(part.shape[0] * 64, 64)

    def pack(value):
        value = value.astype(BF16).reshape(2, 64, 64)
        return jnp.concatenate([value[:, 0:32], value[:, 32:64]], axis=2)

    def head_parts(l):
        both = R.qr[l, :, 0:64, :].reshape(LENGTH, 128)
        q = unpack(R.qr[l, :, 64:96, :])
        return both[:, 0:64], both[:, 64:128], q * BF16(0.125)

    def logits(l, b, q, keys):
        nk = 128 * (b + 1)
        scores = dot_nt(q[128 * b:nk], keys[:nk]) + R.tb[l, :, 896 - 128 * b:1024]
        row = lax.broadcasted_iota(jnp.int32, (128, nk), 0) + 128 * b
        col = lax.broadcasted_iota(jnp.int32, (128, nk), 1)
        ok = (col <= row) & (R.segc[128 * b:nk, :] == R.segr[:, :nk])
        return jnp.where(ok, scores, -1e30)

    def head_fwd(l):
        got(R.qr.at[l], QKV + l)
        keys, values, q = head_parts(l)
        for b in range(8):
            nk = 128 * (b + 1)
            lg = logits(l, b, q, keys)
            top = jnp.max(lg, axis=1, keepdims=True)
            ex = jnp.exp(lg - top)
            tot = jnp.sum(ex, axis=1, keepdims=True)
            out = dot(ex.astype(BF16), values[:nk]) / tot
            R.os[l, 2 * b:2 * b + 2] = pack(out)
            R.lse[l, 128 * b:nk, :] = top + jnp.log(tot)

        def back(i):
            push(R.os.at[l, i], R.mx.at[c * HEADS + s], MIX + l, l, i, r)
        loop(SHARDS, back)

    def head_bwd(l):
        got(R.dor.at[l], DOUT + l)
        keys, values, q = head_parts(l)
        dor, dks, dkv, gg = R.dor, R.dks, R.dkv, R.gg
        dkv[...] = jnp.zeros(dkv.shape, F32)
        gg[...] = jnp.zeros(gg.shape, F32)
        for b in range(8):
            nk = 128 * (b + 1)
            qb = q[128 * b:nk]
            prob = jnp.exp(logits(l, b, q, keys) - R.lse[l, 128 * b:nk, :])
            do = unpack(dor[l, 2 * b:2 * b + 2])
            dp = dot_nt(do, values[:nk])
            delta = jnp.sum(prob * dp, axis=1, keepdims=True)
            dlog = prob * (dp - delta)
            gg[:, 896 - 128 * b:1024] += dlog
            low = dlog.astype(BF16)
            dq = dot(low, keys[:nk]) * 0.125
            dks[l, 2 * b:2 * b + 2, 64:96, :] = pack(dq)
            dkv[:nk, 0:64] += dot_tn(low, qb)
            dkv[:nk, 64:128] += dot_tn(prob.astype(BF16), do)
        dks[l, :, 0:64, :] = dkv[...].astype(BF16).reshape(16, 64, 128)

        def back(i):
            push(dks.at[l, i], R.dkr.at[c * HEADS + s], DQKV + l, l, i, r)
        loop(SHARDS, back)
        flip = (lax.broadcasted_iota(jnp.int32, (128, 128), 0) + lax.broadcasted_iota(jnp.int32, (128, 128), 1)) == 127
        band = dot(flip.astype(F32), gg[...], precision=HIGH)
        band = pltpu.roll(band, 0, 1, stride=1, stride_axis=0)
        diag = jnp.sum(band, axis=0, keepdims=True)
        tg = dot_nt(jnp.broadcast_to(diag, (8, BAND)), R.oh[...].astype(F32), precision=HIGH)
        sub = lax.broadcasted_iota(jnp.int32, (8, 128), 0)
        tg = jnp.where(sub == 2 + s // 2, pltpu.roll(tg, (s % 2) * 64, 1), 0.0)
        R.gts[l] = tg

        def back_table(i):
            push(R.gts.at[l], R.gtr.at[c * HEADS + s], GTAB, l, i, r)
        loop(SHARDS, back_table)

    def norm(x):
        return x * lax.rsqrt(jnp.mean(x * x, axis=1, keepdims=True) + 1e-06)

    def norm_back(x, gain, dn):
        rstd = lax.rsqrt(jnp.mean(x * x, axis=1, keepdims=True) + 1e-06)
        n = x * rstd
        dgain = jnp.sum(dn * n, axis=0, keepdims=True)
        dng = dn * gain
        return rstd * (dng - n * jnp.mean(dng * n, axis=1, keepdims=True)), dgain

    def spread(buf, dst, i, l):
        def step(k):
            push(buf.at[k], dst.at[e], i, l, k // REPLICAS, k % REPLICAS)
        loop(EXPERTS, step)

    def slots(value):
        return value.reshape(EXPERTS, SLOTS, D).astype(BF16)

    def flat(ref):
        return ref[...].astype(F32).reshape(SLOT_ROWS, D).astype(BF16)

    def to_heads(buf, dst, i):
        def step(u):
            push(buf.at[u], dst.at[s], i, u // HEADS, u % HEADS, r)
        loop(24, step)

    def tile(t):
        return pl.ds(pl.multiple_of(t * TILE, TILE), TILE)

    def layer_in(l):
        return R.tok[...] if l == 0 else R.xin[...]

    def wa():
        return ga[...].reshape(D, HALF)

    def wb():
        return gb[...].reshape(D, HALF)

    def wo():
        return gw[...].reshape(D, D)

    def expert_out():
        for t in range(3):
            at = slice(256 * t, 256 * t + 256)
            R.rs[:, :, at] = dot(R.act[...], R.wout[:, at]).reshape(EXPERTS, SLOTS, 256).astype(BF16)

    def expert_back(l):
        for t in range(3):
            at = slice(256 * t, 256 * t + 256)
            R.es[:, :, at] = dot_nt(R.dg[...], R.win[at, :]).reshape(EXPERTS, SLOTS, 256).astype(BF16)
        spread(R.es, R.er, DEXP, l)

    def combine():
        got(R.rr, RET)
        back = flat(R.rr)
        out = R.hidden[...] + dot(R.gth[...], back) + dot(R.gtl[...], back)
        R.acts[...] = out.astype(BF16)
        return out.astype(BF16)

    def send_dy(g, l):
        R.ys[...] = slots(dot(R.gh[...], g) + dot(R.gl[...], g))
        spread(R.ys, R.yr, DY, l)

    def fwd_one(l):
        if l == 1:
            got(R.xin, XPASS)
            gather_end()
        x = layer_in(l).astype(F32)
        nrm = (norm(x) * R.gains[0:1, :]).astype(BF16)
        R.nrm[...] = nrm
        qkv = jnp.concatenate([dot(nrm, wa()).astype(BF16), dot(nrm, wb()).astype(BF16)], axis=1)
        qs = R.qs
        for u in range(24):
            at = 64 * (u // HEADS)
            h = 64 * (u % HEADS)
            qs[u, 0:64, 0:64] = qkv[at:at + 64, D + h:D + h + 64]
            qs[u, 0:64, 64:128] = qkv[at:at + 64, 2 * D + h:2 * D + h + 64]
            qs[u, 64:96, 0:64] = qkv[at:at + 32, h:h + 64]
            qs[u, 64:96, 64:128] = qkv[at + 32:at + 64, h:h + 64]
        to_heads(qs, R.qr.at[l], QKV + l)

    def fwd_two(l):
        got(R.mx, MIX + l)
        mx, mixed = R.mx, R.mixed
        for u in range(24):
            at = 64 * (u // HEADS)
            h = 64 * (u % HEADS)
            mixed[at:at + 32, h:h + 64] = mx[u, :, 0:64]
            mixed[at + 32:at + 64, h:h + 64] = mx[u, :, 64:128]
        got(gw, GW)
        hidden = layer_in(l).astype(F32) + dot(mixed[...], wo())
        R.hidden[...] = hidden
        nrm2 = (norm(hidden) * R.gains[1:2, :]).astype(BF16)
        R.ds[...] = slots(dot(R.smat[...], nrm2))
        spread(R.ds, R.dr, DISP, l)

        got(R.win, WIN)
        got(R.wout, WOUT)
        got(R.dr, DISP)
        rows, win, wout = R.rows, R.win, R.wout
        rows[...] = flat(R.dr)
        if l == 1:
            got(R.yr, DY)
            R.dyrows[...] = flat(R.yr)

            def both(t):
                at = tile(t)
                pre = dot(rows[...], win[:, at])
                dact = dot_nt(R.dyrows[...], wout[at, :])
                sq = pre * pre
                half = 0.5 + 0.5 * jnp.tanh(pre * (C0 + C1 * sq))
                slope = half + pre * (half * (1.0 - half)) * (2.0 * C0 + 6.0 * C1 * sq)
                R.act[:, at] = (pre * half).astype(BF16)
                R.dg[:, at] = (dact * slope).astype(BF16)
            loop(FF // TILE, both)
            expert_back(l)
            expert_out()
            return

        def ffn(t):
            at = tile(t)
            pre = dot(rows[...], win[:, at])
            half = 0.5 + 0.5 * jnp.tanh(pre * (C0 + C1 * (pre * pre)))
            R.act[:, at] = (pre * half).astype(BF16)
        loop(FF // TILE, ffn)
        expert_out()
        spread(R.rs, R.rr, RET, l)

        def slope(t):
            at = tile(t)
            pre = dot(rows[...], win[:, at])
            sq = pre * pre
            half = 0.5 + 0.5 * jnp.tanh(pre * (C0 + C1 * sq))
            R.dg[:, at] = (half + pre * (half * (1.0 - half)) * (2.0 * C0 + 6.0 * C1 * sq)).astype(BF16)
        loop(FF // TILE, slope)
        out = combine()
        R.xsend[...] = out
        send(R.xsend, R.xin, XPASS, 1, s, r)

    def bwd_one(l):
        if l == 0:
            got(R.gin, GPASS)
        g = R.cot[...] if l == 1 else R.gin[...]
        rows, win, wout, act, dg, dyrows = R.rows, R.win, R.wout, R.act, R.dg, R.dyrows
        if l == 0:
            send_dy(g, l)
            got(R.yr, DY)
            dyrows[...] = flat(R.yr)

            def ffn(t):
                at = tile(t)
                dact = dot_nt(dyrows[...], wout[at, :])
                dg[:, at] = (dact * dg[:, at].astype(F32)).astype(BF16)
            loop(FF // TILE, ffn)
            expert_back(l)

        def weights(t):
            at = tile(t)
            win[:, at] = dot_tn(rows[...], dg[:, at]).astype(BF16)
            wout[at, :] = dot_tn(act[:, at], dyrows[...]).astype(BF16)
        loop(FF // TILE, weights)
        pltpu.make_async_copy(win, R.gwin, rsem.at[OWIN]).start()
        pltpu.make_async_copy(wout, R.gwout, rsem.at[OWOUT]).start()

        got(R.er, DEXP)
        dn2 = dot(R.stmat[...], flat(R.er))
        dx, dgain = norm_back(R.hidden[...], R.gains[1:2, :], dn2)
        R.sm[...] = jnp.zeros((8, D), F32)
        R.sm[1:2, :] = dgain
        dh = g.astype(F32) + dx
        R.dh[...] = dh
        dattn = dh.astype(BF16)
        dmix = dot_nt(dattn, wo()).astype(BF16)
        dos = R.dos
        for u in range(24):
            at = 64 * (u // HEADS)
            h = 64 * (u % HEADS)
            dos[u, :, 0:64] = dmix[at:at + 32, h:h + 64]
            dos[u, :, 64:128] = dmix[at + 32:at + 64, h:h + 64]
        to_heads(dos, R.dor.at[l], DOUT + l)
        if l == 1:
            spread(R.rs, R.rr, RET, l)
        gout = dot_tn(R.mixed[...], dattn)
        R.gop[...] = gout.astype(BF16).reshape(16, 48, D)

        def reduce_out(i):
            push(R.gop.at[i], R.gor.at[s], GO, l, i, r)
        loop(SHARDS, reduce_out)

    def bwd_two(l):
        got(R.dkr, DQKV + l)
        dkr, dqkv, gp = R.dkr, R.dqkv, R.gp
        for u in range(24):
            at = 64 * (u // HEADS)
            h = 64 * (u % HEADS)
            dqkv[at:at + 64, D + h:D + h + 64] = dkr[u, 0:64, 0:64]
            dqkv[at:at + 64, 2 * D + h:2 * D + h + 64] = dkr[u, 0:64, 64:128]
            dqkv[at:at + 32, h:h + 64] = dkr[u, 64:96, 0:64]
            dqkv[at + 32:at + 64, h:h + 64] = dkr[u, 64:96, 64:128]
        nrm = R.nrm
        def part(t):
            at = slice(384 * t, 384 * t + 384)
            gp[:, :, :, at] = dot_tn(nrm[...], dqkv[:, at]).astype(BF16).reshape(4, 4, 48, 384)

        def reduce_a(i):
            push(gp.at[:, i, :, pl.ds(0, HALF)], R.r1a.at[z], RA1, l, y * 4 + i, r)

        def reduce_b(i):
            push(gp.at[i, :, :, pl.ds(HALF, HALF)], R.r1b.at[y], RB1, l, i * 4 + z, r)
        for t in range(3):
            part(t)
        loop(4, reduce_a)
        for t in range(3, 6):
            part(t)
        loop(4, reduce_b)
        dn = dot_nt(dqkv[:, 0:HALF], wa()) + dot_nt(dqkv[:, HALF:2 * HALF], wb())
        dx, dgain = norm_back(layer_in(l).astype(F32), R.gains[0:1, :], dn)
        low = (R.dh[...] + dx).astype(BF16)
        R.sgr[...] = low
        if l == 1:
            R.xsend[...] = low
            send(R.xsend, R.gin, GPASS, 0, s, r)
        R.sm[0:1, :] = dgain

        if l == 1:
            combine()

        def reduce_small(i):
            push(R.sm, R.smr.at[s], SMALL, l, i, r)
        loop(SHARDS, reduce_small)

    def reduce(l):
        r1a, r1b, r2a, r2b, gx, sx = (R.r1a, R.r1b, R.r2a, R.r2b, R.gx, R.sx)

        def four(ref, at):
            return ref[(0,) + at].astype(F32) + ref[(1,) + at].astype(F32) + ref[(2,) + at].astype(F32) + ref[(3,) + at].astype(F32)

        got(r1a, RA1)
        got(r1b, RB1)
        for k in range(4):
            R.p2a[k] = four(r1a, (k,)).astype(BF16)
            R.p2b[k] = four(r1b, (k,)).astype(BF16)

        def reduce_two(i):
            push(R.p2a.at[i], r2a.at[y], RA2, l, i * 4 + z, r)
            push(R.p2b.at[i], r2b.at[z], RB2, l, y * 4 + i, r)
        loop(4, reduce_two)

        got(R.gor, GO)
        part = R.gor[0].astype(F32)
        for k in range(1, SHARDS):
            part = part + R.gor[k].astype(F32)
        R.gxs[:, 2304:3072] = part.astype(BF16)
        got(R.smr, SMALL)
        got(R.gtr, GTAB)
        small = R.smr[0]
        for k in range(1, SHARDS):
            small = small + R.smr[k]
        table = R.gtr[0]
        for k in range(1, 24):
            table = table + R.gtr[k]
        R.sxs[...] = small + jnp.concatenate([table, jnp.zeros((8, D - 128), F32)], axis=1)
        got(r2a, RA2)
        got(r2b, RB2)
        R.gxs[:, 0:HALF] = four(r2a, ()).astype(BF16)
        R.gxs[:, HALF:2 * HALF] = four(r2b, ()).astype(BF16)

        def over_replicas(i):
            push(R.gxs, gx.at[r], GX, c, s, i)
            push(R.sxs, sx.at[r], SX, c, s, i)
        loop(REPLICAS, over_replicas)
        got(gx, GX)
        got(sx, SX)
        grads = four(gx, ()).astype(BF16)
        R.gqkv[...] = grads[:, 0:2304]
        R.gout[...] = grads[:, 2304:3072]
        total = four(sx, ())
        mine = pltpu.roll(total, lax.rem(D - 48 * s, D), 1)
        R.ggain1[...] = mine[0:1, 0:48].astype(BF16)
        R.ggain2[...] = mine[1:2, 0:48].astype(BF16)
        rows = pltpu.roll(total[:, 0:128], lax.rem(128 - 2 * s, 128), 1)
        sent(mr.at[pl.ds(0, 31)], MISC)
        spare = R.misc
        for k in range(2):
            for h in range(HEADS):
                at = (h % 2) * 64 + k
                spare[k:k + 1, h:h + 1] = rows[2 + h // 2:3 + h // 2, at:at + 1]
        R.gtable[...] = spare[0:2, 0:HEADS].astype(BF16)

    for l in range(2):
        pl.when(c == l)(lambda l=l: fwd_one(l))
        if l == 0:
            pl.when((c == 0) & is_head)(set_heads)
        pl.when(is_head)(lambda l=l: head_fwd(l))
        if l == 0:
            set_routes()
            pl.when(c == 1)(lambda: send_dy(R.cot[...], 1))
        pl.when(c == l)(lambda l=l: fwd_two(l))
    for l in (1, 0):
        pl.when(c == l)(lambda l=l: bwd_one(l))
        pl.when(is_head)(lambda l=l: head_bwd(l))
        pl.when(c == l)(lambda l=l: bwd_two(l))
        pl.when(c == l)(lambda l=l: reduce(l))

    sent(ga.at[0, pl.ds(0, 3)], GA1)
    sent(gb.at[0, pl.ds(0, 3)], GB1)
    sent(ga.at[pl.ds(0, 3)], GA2)
    sent(gb.at[pl.ds(0, 3)], GB2)
    few = EXPERTS - 1
    sent(R.ds.at[pl.ds(0, few)], DISP)
    sent(R.rs.at[pl.ds(0, few)], RET)
    sent(R.ys.at[pl.ds(0, few)], DY)
    sent(R.es.at[pl.ds(0, few)], DEXP)
    sent(gw.at[pl.ds(0, 15)], GW)
    sent(R.gop.at[pl.ds(0, 15)], GO)
    sent(R.r1a.at[pl.ds(0, 3)], RA1)
    sent(R.r1b.at[pl.ds(0, 3)], RB1)
    sent(R.p2a.at[pl.ds(0, 3)], RA2)
    sent(R.p2b.at[pl.ds(0, 3)], RB2)
    sent(R.smr.at[pl.ds(0, 15)], SMALL)
    sent(R.gx.at[pl.ds(0, 3)], GX)
    sent(R.sx.at[pl.ds(0, 3)], SX)
    got(R.win, OWIN)
    got(R.wout, OWOUT)
    for l in range(2):
        @pl.when(c == l)
        def _():
            sent(R.xsend, XPASS if l == 0 else GPASS)
            for buf, i in ((R.qs, QKV + l), (R.dos, DOUT + l)):
                pl.when(is_head)(lambda buf=buf, i=i: sent(buf.at[pl.ds(0, 23)], i))
                pl.when(jnp.logical_not(is_head))(lambda buf=buf, i=i: sent(buf, i))

        @pl.when(is_head)
        def _():
            for buf, i in ((R.os, MIX + l), (R.dks, DQKV + l)):
                pl.when(c == l)(lambda buf=buf, i=i: sent(buf.at[l, pl.ds(0, 15)], i))
                pl.when(c != l)(lambda buf=buf, i=i: sent(buf.at[l], i))

    @pl.when(is_head)
    def _():
        sent(mr.at[pl.ds(0, 31)], GTAB)


def settle(*refs):
    ins, outs, held, sems = refs[:9], refs[9:18], refs[18:27], refs[27]
    pieces = [(i, pl.ds(0, ins[i].shape[0])) for i in range(7)]
    for i in (7, 8):
        step = ins[i].shape[0] // 6
        pieces += [(i, pl.ds(k * step, step)) for k in range(6)]
    into = [pltpu.make_async_copy(ins[i].at[at], held[i].at[at], sems.at[0, n]) for n, (i, at) in enumerate(pieces)]
    out = [pltpu.make_async_copy(held[i].at[at], outs[i].at[at], sems.at[1, n]) for n, (i, at) in enumerate(pieces)]
    for copy in into:
        copy.start()
    for first, second in zip(into, out):
        first.wait()
        second.start()
    for copy in out:
        copy.wait()


def body(tokens, cotangent, wqkv, wout, gain_attn, gain_ffn, rel_table, w_in, w_out_exp, expert_ids, gates, seg_ids, buckets):
    vmem = pl.BlockSpec(memory_space=pltpu.VMEM)
    hbm = pl.BlockSpec(memory_space=pl.ANY)
    shapes = ((TOK, D), (TOK, D), (48, 2304), (48, D), (1, 48), (1, 48), (2, HEADS), (D, FF), (FF, D))
    shapes = tuple(jax.ShapeDtypeStruct(v, BF16) for v in shapes)
    scratch = [pltpu.VMEM(*v) for v in SCRATCH.values()]
    outs = pl.pallas_call(
        kernel,
        out_shape=shapes,
        in_specs=[vmem] * 11 + [hbm] * 2,
        out_specs=(vmem,) * 7 + (hbm, hbm),
        scratch_shapes=scratch + [pltpu.SemaphoreType.DMA((33,)), pltpu.SemaphoreType.DMA((33,)), pltpu.SemaphoreType.REGULAR],
        compiler_params=pltpu.CompilerParams(has_side_effects=True, vmem_limit_bytes=64 * 1024 * 1024 - 65536),
        name="relay",
    )(tokens.reshape(TOK, D), cotangent.reshape(TOK, D), wqkv[0], wout[0], gain_attn, gain_ffn, rel_table[0],
      expert_ids.reshape(TOK, 2), gates.reshape(TOK, 2), seg_ids, buckets[None, :], w_in[0, 0], w_out_exp[0, 0])
    outs = pl.pallas_call(
        settle,
        out_shape=shapes,
        in_specs=[hbm] * 9,
        out_specs=(hbm,) * 9,
        scratch_shapes=[pltpu.VMEM(v.shape, BF16) for v in shapes] + [pltpu.SemaphoreType.DMA((2, 19))],
        compiler_params=pltpu.CompilerParams(vmem_limit_bytes=56 * 1024 * 1024),
        name="settle",
    )(*outs)
    acts, sgr, gqkv, gout, ggain1, ggain2, gtable, gwin, gwout = outs
    return (
        acts.reshape(1, 2, ROWS, D),
        sgr.reshape(1, 2, ROWS, D),
        gqkv[None],
        gout[None],
        ggain1,
        ggain2,
        gtable[None],
        gwin[None, None],
        gwout[None, None],
    )


def solution(mesh):
    in_specs = (
        P("replica", "shard", None),
        P("replica", "shard", None),
        P("section", "shard", None),
        P("section", "shard", None),
        P("section", "shard"),
        P("section", "shard"),
        P("section", "shard", None),
        P("section", ("shard", "replica"), None, None),
        P("section", ("shard", "replica"), None, None),
        P("section", "replica", "shard", None),
        P("section", "replica", "shard", None),
        P("replica", None),
        P(),
    )
    out_specs = (
        P("section", "replica", "shard", None),
        P("section", "replica", "shard", None),
        P("section", "shard", None),
        P("section", "shard", None),
        P("section", "shard"),
        P("section", "shard"),
        P("section", "shard", None),
        P("section", ("shard", "replica"), None, None),
        P("section", ("shard", "replica"), None, None),
    )
    return jax.shard_map(body, mesh=mesh, in_specs=in_specs, out_specs=out_specs, check_vma=False)
```

```python
from types import SimpleNamespace

import jax
import jax.numpy as jnp
from jax import lax
from jax.experimental import pallas as pl
from jax.experimental.pallas import tpu as pltpu
from jax.sharding import PartitionSpec as P

MESH = pl.DeviceIdType.MESH
F32 = jnp.float32
BF16 = jnp.bfloat16
HIGH = lax.Precision.HIGHEST

D, HEADS, HD, FF = 768, 12, 64, 3072
LENGTH, ROWS, EXPERTS, SLOTS = 1024, 64, 64, 8
SHARDS, REPLICAS = 16, 4
TOK = 2 * ROWS
SLOT_ROWS = EXPERTS * SLOTS
BAND = LENGTH + 128
TILE = 512
HALF = 1152
C0 = 0.7978845608028654
C1 = C0 * 0.044715

MISC, GA1, GB1, GA2, GB2 = 0, 1, 2, 3, 4
QKV, MIX, DOUT, DQKV = 6, 8, 10, 12
DISP, RET, DY, DEXP, XPASS, GPASS = 14, 15, 16, 17, 18, 19
GTAB, SMALL, GO, GX, SX = 20, 21, 22, 23, 24
WIN, WOUT, OWIN, OWOUT = 25, 26, 27, 28
GW, RA1, RB1, RA2, RB2, GOX = 5, 29, 30, 31, 32, 33

SCRATCH = dict(
    ga=((4, 4, 48, HALF), BF16),
    gb=((4, 4, 48, HALF), BF16),
    gw=((16, 48, D), BF16),
    misc=((8, 128), F32),
    mr=((32, 8, 128), F32),
    gains=((8, D), F32),
    oh=((128, BAND), BF16),
    segr=((1, LENGTH), F32),
    segc=((LENGTH, 1), F32),
    smat=((SLOT_ROWS, TOK), BF16),
    gh=((SLOT_ROWS, TOK), BF16),
    gl=((SLOT_ROWS, TOK), BF16),
    stmat=((TOK, SLOT_ROWS), BF16),
    gth=((TOK, SLOT_ROWS), BF16),
    gtl=((TOK, SLOT_ROWS), BF16),
    tb=((2, 128, LENGTH), F32),
    gg=((128, BAND), F32),
    win=((D, FF), BF16),
    wout=((FF, D), BF16),
    qs=((24, 96, 128), BF16),
    qr=((2, 16, 96, 128), BF16),
    os=((2, 16, 32, 128), BF16),
    mx=((24, 32, 128), BF16),
    mixed=((TOK, D), BF16),
    nrm=((TOK, D), BF16),
    hidden=((TOK, D), F32),
    xsend=((TOK, D), BF16),
    xin=((TOK, D), BF16),
    gin=((TOK, D), BF16),
    ds=((EXPERTS, SLOTS, D), BF16),
    dr=((EXPERTS, SLOTS, D), BF16),
    rs=((EXPERTS, SLOTS, D), BF16),
    rr=((EXPERTS, SLOTS, D), BF16),
    ys=((EXPERTS, SLOTS, D), BF16),
    yr=((EXPERTS, SLOTS, D), BF16),
    es=((EXPERTS, SLOTS, D), BF16),
    er=((EXPERTS, SLOTS, D), BF16),
    rows=((SLOT_ROWS, D), BF16),
    dyrows=((SLOT_ROWS, D), BF16),
    act=((SLOT_ROWS, FF), BF16),
    dg=((SLOT_ROWS, FF), BF16),
    lse=((2, LENGTH, 1), F32),
    dos=((24, 32, 128), BF16),
    dor=((2, 16, 32, 128), BF16),
    dks=((2, 16, 96, 128), BF16),
    dkr=((24, 96, 128), BF16),
    dkv=((LENGTH, 128), F32),
    dqkv=((TOK, 2304), BF16),
    dh=((TOK, D), F32),
    gp=((4, 4, 48, 2304), BF16),
    r1a=((4, 4, 48, HALF), BF16),
    r1b=((4, 4, 48, HALF), BF16),
    p2a=((4, 48, HALF), BF16),
    p2b=((4, 48, HALF), BF16),
    r2a=((4, 48, HALF), BF16),
    r2b=((4, 48, HALF), BF16),
    gop=((16, 48, D), BF16),
    gor=((16, 48, D), BF16),
    gxs=((48, 2304), BF16),
    gx=((4, 48, 2304), BF16),
    gos=((48, D), BF16),
    gox=((4, 48, D), BF16),
    sm=((8, D), F32),
    smr=((16, 8, D), F32),
    sxs=((8, D), F32),
    sx=((4, 8, D), F32),
    gts=((2, 8, 128), F32),
    gtr=((24, 8, 128), F32),
)
INPUTS = dict(tok=0, cot=0, wq=0, wo=0, gain1=0, gain2=0, table=0, ids=0, gate=0, seg=0, bk=0, winh=0, wouth=0)
OUTPUTS = dict(acts=0, sgr=0, gqkv=0, gout=0, ggain1=0, ggain2=0, gtable=0, gwin=0, gwout=0)


def dot(a, b, **kw):
    return jnp.dot(a, b, preferred_element_type=F32, **kw)


def dot_nt(a, b, **kw):
    return lax.dot_general(a, b, (((1,), (1,)), ((), ())), preferred_element_type=F32, **kw)


def dot_tn(a, b, **kw):
    return lax.dot_general(a, b, (((0,), (0,)), ((), ())), preferred_element_type=F32, **kw)


def loop(count, step):
    def wrapped(i, carry):
        step(i)
        return carry
    lax.fori_loop(0, count, wrapped, 0)


def kernel(*refs):
    names = tuple(INPUTS) + tuple(OUTPUTS) + tuple(SCRATCH)
    R = SimpleNamespace(**dict(zip(names, refs)))
    ssem, rsem, go = refs[len(names):]
    c = lax.axis_index("section")
    s = lax.axis_index("shard")
    r = lax.axis_index("replica")
    e = s * REPLICAS + r
    y = s // 4
    z = s % 4

    def push(src, dst, i, tc, ts, tr):
        same = (tc == c) & (ts == s) & (tr == r)

        @pl.when(same)
        def _():
            pltpu.make_async_copy(src, dst, rsem.at[i]).start()

        @pl.when(jnp.logical_not(same))
        def _():
            send(src, dst, i, tc, ts, tr)

    def send(src, dst, i, tc, ts, tr):
        pltpu.make_async_remote_copy(
            src_ref=src, dst_ref=dst, send_sem=ssem.at[i], recv_sem=rsem.at[i],
            device_id=(tc, ts, tr), device_id_type=MESH,
        ).start()

    def far(j):
        return jnp.where(j == 0, 2, jnp.where(j == 1, 1, jnp.where(j == 2, 3, 0)))

    def far_shard(j):
        return (y + far(j // 4)) % 4 * 4 + (z + far(j % 4)) % 4

    def got(ref, i):
        pltpu.make_async_copy(ref, ref, rsem.at[i]).wait()

    def sent(ref, i):
        pltpu.make_async_copy(ref, ref, ssem.at[i]).wait()

    pltpu.make_async_copy(R.winh, R.win, rsem.at[WIN]).start()
    pltpu.make_async_copy(R.wouth, R.wout, rsem.at[WOUT]).start()

    wq, ga, gb, gw = R.wq, R.ga, R.gb, R.gw

    def gather_one(i):
        push(wq.at[:, pl.ds(0, HALF)], ga.at[y, z], GA1, c, y * 4 + i, r)
        push(wq.at[:, pl.ds(HALF, HALF)], gb.at[y, z], GB1, c, i * 4 + z, r)

    def gather_two(i):
        @pl.when(i != y)
        def _():
            send(ga.at[y], ga.at[y], GA2, c, i * 4 + z, r)

        @pl.when(i != z)
        def _():
            send(gb.at[:, z], gb.at[:, z], GB2, c, y * 4 + i, r)

    def gather_out(i):
        push(R.wo, gw.at[s], GW, c, i, r)

    def gather_start():
        loop(4, gather_one)

    def gather_middle():
        got(ga.at[y], GA1)
        got(gb.at[:, z], GB1)
        loop(4, gather_two)

    def gather_end():
        got(ga.at[pl.ds(0, 3)], GA2)
        got(gb.at[pl.ds(0, 3)], GB2)

    pl.when(c == 0)(gather_start)

    misc = R.misc
    misc[...] = jnp.zeros(misc.shape, F32)
    misc[0:1, 0:48] = R.gain1[...].astype(F32)
    misc[1:2, 0:48] = R.gain2[...].astype(F32)
    table = R.table[...].astype(F32)
    for k in range(2):
        for h in range(HEADS):
            at = (h % 2) * 64 + k
            misc[2 + h // 2:3 + h // 2, at:at + 1] = table[k:k + 1, h:h + 1]

    def misc_step(i):
        push(misc, R.mr.at[c * 16 + s], MISC, i // 16, i % 16, r)
    loop(32, misc_step)

    pl.when(c == 0)(gather_middle)

    r128 = lax.broadcasted_iota(jnp.int32, (TOK, TOK), 0)
    c128 = lax.broadcasted_iota(jnp.int32, (TOK, TOK), 1)
    eye = r128 == c128

    def column(row):
        return jnp.sum(jnp.where(eye, row, 0.0), axis=1, keepdims=True)

    def lay(col):
        return jnp.sum(jnp.where(eye, col, 0.0), axis=0, keepdims=True)
    got(R.mr, MISC)
    mr = R.mr
    lane = lax.broadcasted_iota(jnp.int32, (8, D), 1)
    total = jnp.zeros((8, D), F32)
    for k in range(SHARDS):
        piece = jnp.concatenate([mr[c * 16 + k], jnp.zeros((8, D - 128), F32)], axis=1)
        piece = jnp.where(lane < 48, piece, 0.0)
        total = total + (pltpu.roll(piece, 48 * k, 1) if k else piece)
    R.gains[...] = total

    is_head = s < HEADS

    def set_routes():
        id_cols = [R.ids[:, k:k + 1].astype(F32) for k in range(2)]
        gate_cols = [R.gate[:, k:k + 1] for k in range(2)]
        id_rows = [lay(v) for v in id_cols]
        gate_rows = [lay(v) for v in gate_cols]
        before = (c128 < r128) & (c128 // ROWS == r128 // ROWS)
        slot_cols = []
        for k in range(2):
            own = id_cols[k]
            same = (own == id_rows[0]).astype(F32) + (own == id_rows[1]).astype(F32)
            rank = jnp.sum(jnp.where(before, same, 0.0), axis=1, keepdims=True)
            part = (lax.broadcasted_iota(jnp.int32, (TOK, 1), 0) // ROWS * 3).astype(F32)
            slot_cols.append(own * SLOTS + part + rank)
        down = lax.broadcasted_iota(jnp.int32, (SLOT_ROWS, TOK), 0).astype(F32)
        across = lax.broadcasted_iota(jnp.int32, (TOK, SLOT_ROWS), 1).astype(F32)

        def matrices(hits, gates, refs):
            full = jnp.where(hits[0], gates[0], 0.0) + jnp.where(hits[1], gates[1], 0.0)
            high = full.astype(BF16)
            refs[0][...] = (hits[0] | hits[1]).astype(F32).astype(BF16)
            refs[1][...] = high
            refs[2][...] = (full - high.astype(F32)).astype(BF16)
        matrices([lay(v) == down for v in slot_cols], gate_rows, (R.smat, R.gh, R.gl))
        matrices([v == across for v in slot_cols], gate_cols, (R.stmat, R.gth, R.gtl))

    def set_heads():
        seg = R.seg[...].astype(F32)
        R.segr[...] = jnp.where(c == 0, seg[0:1, :], seg[1:2, :])
        for b in range(8):
            R.segc[128 * b:128 * b + 128, :] = column(R.segr[:, 128 * b:128 * b + 128])
        R.oh[...] = jnp.zeros((128, BAND), BF16)
        bk = jnp.broadcast_to(R.bk[...], (8, LENGTH)).astype(F32).astype(BF16)
        turn = (r128 + c128 == 127).astype(F32).astype(BF16)
        bk = jnp.concatenate([dot(bk[:, 896 - 128 * k:1024 - 128 * k], turn) for k in range(8)], axis=1)[0:1, :]
        R.oh[:, 0:LENGTH] = (bk.astype(jnp.int32) == lax.broadcasted_iota(jnp.int32, (128, LENGTH), 0)).astype(F32).astype(BF16)

        sub = lax.broadcasted_iota(jnp.int32, (8, 128), 0)
        for l in range(2):
            tab = jnp.zeros((8, 128), F32)
            for k in range(SHARDS):
                tab = tab + (pltpu.roll(mr[l * 16 + k], 2 * k, 1) if k else mr[l * 16 + k])
            tab = jnp.where(sub == 2 + s // 2, tab, 0.0)
            tab = pltpu.roll(tab, (s % 2) * 64, 1)
            row = jnp.sum(tab, axis=0, keepdims=True)
            base = dot(jnp.broadcast_to(row, (8, 128)).astype(BF16), R.oh[...])
            band = jnp.broadcast_to(base[0:1], (128, BAND))
            band = pltpu.roll(band, BAND - 127, 1, stride=1, stride_axis=0)
            R.tb[l] = band[:, :LENGTH]

    @pl.when(c == 0)
    def _():
        gather_end()
        pl.semaphore_signal(go, 1, device_id=(1, s, r), device_id_type=MESH)

    pl.when((c == 1) & is_head)(set_heads)

    @pl.when(c == 1)
    def _():
        pl.semaphore_wait(go, 1)
        gather_start()
        gather_middle()
    loop(SHARDS, gather_out)

    def unpack(part):
        return jnp.concatenate([part[:, :, 0:64], part[:, :, 64:128]], axis=1).reshape(part.shape[0] * 64, 64)

    def pack(value):
        value = value.astype(BF16).reshape(2, 64, 64)
        return jnp.concatenate([value[:, 0:32], value[:, 32:64]], axis=2)

    def head_parts(l):
        both = R.qr[l, :, 0:64, :].reshape(LENGTH, 128)
        q = unpack(R.qr[l, :, 64:96, :])
        return both[:, 0:64], both[:, 64:128], q * BF16(0.125)

    def logits(l, b, q, keys):
        nk = 128 * (b + 1)
        scores = dot_nt(q[128 * b:nk], keys[:nk]) + R.tb[l, :, 896 - 128 * b:1024]
        row = lax.broadcasted_iota(jnp.int32, (128, nk), 0) + 128 * b
        col = lax.broadcasted_iota(jnp.int32, (128, nk), 1)
        ok = (col <= row) & (R.segc[128 * b:nk, :] == R.segr[:, :nk])
        return jnp.where(ok, scores, -1e30)

    def head_fwd(l):
        got(R.qr.at[l], QKV + l)
        keys, values, q = head_parts(l)
        for b in range(8):
            nk = 128 * (b + 1)
            lg = logits(l, b, q, keys)
            top = jnp.max(lg, axis=1, keepdims=True)
            ex = jnp.exp(lg - top)
            tot = jnp.sum(ex, axis=1, keepdims=True)
            out = dot(ex.astype(BF16), values[:nk]) / tot
            R.os[l, 2 * b:2 * b + 2] = pack(out)
            R.lse[l, 128 * b:nk, :] = top + jnp.log(tot)

        def back(k):
            i = far_shard(k)
            push(R.os.at[l, i], R.mx.at[c * HEADS + s], MIX + l, l, i, r)
        loop(SHARDS, back)

    def head_bwd(l):
        got(R.dor.at[l], DOUT + l)
        keys, values, q = head_parts(l)
        dor, dks, dkv, gg = R.dor, R.dks, R.dkv, R.gg
        dkv[...] = jnp.zeros(dkv.shape, F32)
        gg[...] = jnp.zeros(gg.shape, F32)
        for b in range(8):
            nk = 128 * (b + 1)
            qb = q[128 * b:nk]
            prob = jnp.exp(logits(l, b, q, keys) - R.lse[l, 128 * b:nk, :])
            do = unpack(dor[l, 2 * b:2 * b + 2])
            dp = dot_nt(do, values[:nk])
            delta = jnp.sum(prob * dp, axis=1, keepdims=True)
            dlog = prob * (dp - delta)
            gg[:, 896 - 128 * b:1024] += dlog
            low = dlog.astype(BF16)
            dq = dot(low, keys[:nk]) * 0.125
            dks[l, 2 * b:2 * b + 2, 64:96, :] = pack(dq)
            dkv[:nk, 0:64] += dot_tn(low, qb)
            dkv[:nk, 64:128] += dot_tn(prob.astype(BF16), do)
        dks[l, :, 0:64, :] = dkv[...].astype(BF16).reshape(16, 64, 128)

        def back(k):
            i = far_shard(k)
            push(dks.at[l, i], R.dkr.at[c * HEADS + s], DQKV + l, l, i, r)
        loop(SHARDS, back)
        flip = (lax.broadcasted_iota(jnp.int32, (128, 128), 0) + lax.broadcasted_iota(jnp.int32, (128, 128), 1)) == 127
        band = dot(flip.astype(F32), gg[...], precision=HIGH)
        band = pltpu.roll(band, 0, 1, stride=1, stride_axis=0)
        diag = jnp.sum(band, axis=0, keepdims=True)
        tg = dot_nt(jnp.broadcast_to(diag, (8, BAND)), R.oh[...].astype(F32), precision=HIGH)
        sub = lax.broadcasted_iota(jnp.int32, (8, 128), 0)
        tg = jnp.where(sub == 2 + s // 2, pltpu.roll(tg, (s % 2) * 64, 1), 0.0)
        R.gts[l] = tg

        def back_table(i):
            push(R.gts.at[l], R.gtr.at[c * HEADS + s], GTAB, l, i, r)
        loop(SHARDS, back_table)

    def norm(x):
        return x * lax.rsqrt(jnp.mean(x * x, axis=1, keepdims=True) + 1e-06)

    def norm_back(x, gain, dn):
        rstd = lax.rsqrt(jnp.mean(x * x, axis=1, keepdims=True) + 1e-06)
        n = x * rstd
        dgain = jnp.sum(dn * n, axis=0, keepdims=True)
        dng = dn * gain
        return rstd * (dng - n * jnp.mean(dng * n, axis=1, keepdims=True)), dgain

    def spread(buf, dst, i, l):
        def step(k):
            ts, tr = far_shard(k // REPLICAS), (r + far(k % REPLICAS)) % REPLICAS
            push(buf.at[ts * REPLICAS + tr], dst.at[e], i, l, ts, tr)
        loop(EXPERTS, step)

    def slots(value):
        return value.reshape(EXPERTS, SLOTS, D).astype(BF16)

    def flat(ref):
        return ref[...].astype(F32).reshape(SLOT_ROWS, D).astype(BF16)

    def to_heads(buf, dst, i):
        def step(k):
            h = far_shard(k // 2)

            @pl.when(h < HEADS)
            def _():
                push(buf.at[k % 2 * HEADS + h], dst.at[s], i, k % 2, h, r)
        loop(32, step)

    def tile(t):
        return pl.ds(pl.multiple_of(t * TILE, TILE), TILE)

    def layer_in(l):
        return R.tok[...] if l == 0 else R.xin[...]

    def wa():
        return ga[...].reshape(D, HALF)

    def wb():
        return gb[...].reshape(D, HALF)

    def wo():
        return gw[...].reshape(D, D)

    def expert_out():
        for t in range(3):
            at = slice(256 * t, 256 * t + 256)
            R.rs[:, :, at] = dot(R.act[...], R.wout[:, at]).reshape(EXPERTS, SLOTS, 256).astype(BF16)

    def expert_back(l):
        for t in range(3):
            at = slice(256 * t, 256 * t + 256)
            R.es[:, :, at] = dot_nt(R.dg[...], R.win[at, :]).reshape(EXPERTS, SLOTS, 256).astype(BF16)
        spread(R.es, R.er, DEXP, l)

    def combine():
        got(R.rr, RET)
        back = flat(R.rr)
        out = R.hidden[...] + dot(R.gth[...], back) + dot(R.gtl[...], back)
        R.acts[...] = out.astype(BF16)
        return out.astype(BF16)

    def send_dy(g, l):
        R.ys[...] = slots(dot(R.gh[...], g) + dot(R.gl[...], g))
        spread(R.ys, R.yr, DY, l)

    def fwd_one(l):
        if l == 1:
            got(R.xin, XPASS)
            gather_end()
        x = layer_in(l).astype(F32)
        nrm = (norm(x) * R.gains[0:1, :]).astype(BF16)
        R.nrm[...] = nrm
        qkv = jnp.concatenate([dot(nrm, wa()).astype(BF16), dot(nrm, wb()).astype(BF16)], axis=1)
        qs = R.qs
        for u in range(24):
            at = 64 * (u // HEADS)
            h = 64 * (u % HEADS)
            qs[u, 0:64, 0:64] = qkv[at:at + 64, D + h:D + h + 64]
            qs[u, 0:64, 64:128] = qkv[at:at + 64, 2 * D + h:2 * D + h + 64]
            qs[u, 64:96, 0:64] = qkv[at:at + 32, h:h + 64]
            qs[u, 64:96, 64:128] = qkv[at + 32:at + 64, h:h + 64]
        to_heads(qs, R.qr.at[l], QKV + l)

    def fwd_two(l):
        got(R.mx, MIX + l)
        mx, mixed = R.mx, R.mixed
        for u in range(24):
            at = 64 * (u // HEADS)
            h = 64 * (u % HEADS)
            mixed[at:at + 32, h:h + 64] = mx[u, :, 0:64]
            mixed[at + 32:at + 64, h:h + 64] = mx[u, :, 64:128]
        got(gw, GW)
        hidden = layer_in(l).astype(F32) + dot(mixed[...], wo())
        R.hidden[...] = hidden
        nrm2 = (norm(hidden) * R.gains[1:2, :]).astype(BF16)
        R.ds[...] = slots(dot(R.smat[...], nrm2))
        spread(R.ds, R.dr, DISP, l)

        got(R.win, WIN)
        got(R.wout, WOUT)
        got(R.dr, DISP)
        rows, win, wout = R.rows, R.win, R.wout
        rows[...] = flat(R.dr)
        if l == 1:
            got(R.yr, DY)
            R.dyrows[...] = flat(R.yr)

            def both(t):
                at = tile(t)
                pre = dot(rows[...], win[:, at])
                dact = dot_nt(R.dyrows[...], wout[at, :])
                sq = pre * pre
                half = 0.5 + 0.5 * jnp.tanh(pre * (C0 + C1 * sq))
                slope = half + pre * (half * (1.0 - half)) * (2.0 * C0 + 6.0 * C1 * sq)
                R.act[:, at] = (pre * half).astype(BF16)
                R.dg[:, at] = (dact * slope).astype(BF16)
            loop(FF // TILE, both)
            expert_back(l)
            expert_out()
            return

        def ffn(t):
            at = tile(t)
            pre = dot(rows[...], win[:, at])
            half = 0.5 + 0.5 * jnp.tanh(pre * (C0 + C1 * (pre * pre)))
            R.act[:, at] = (pre * half).astype(BF16)
        loop(FF // TILE, ffn)
        expert_out()
        spread(R.rs, R.rr, RET, l)

        def slope(t):
            at = tile(t)
            pre = dot(rows[...], win[:, at])
            sq = pre * pre
            half = 0.5 + 0.5 * jnp.tanh(pre * (C0 + C1 * sq))
            R.dg[:, at] = (half + pre * (half * (1.0 - half)) * (2.0 * C0 + 6.0 * C1 * sq)).astype(BF16)
        loop(FF // TILE, slope)
        out = combine()
        R.xsend[...] = out
        send(R.xsend, R.xin, XPASS, 1, s, r)

    def bwd_one(l):
        if l == 0:
            got(R.gin, GPASS)
        g = R.cot[...] if l == 1 else R.gin[...]
        rows, win, wout, act, dg, dyrows = R.rows, R.win, R.wout, R.act, R.dg, R.dyrows
        if l == 0:
            send_dy(g, l)
            got(R.yr, DY)
            dyrows[...] = flat(R.yr)

            def ffn(t):
                at = tile(t)
                dact = dot_nt(dyrows[...], wout[at, :])
                dg[:, at] = (dact * dg[:, at].astype(F32)).astype(BF16)
            loop(FF // TILE, ffn)
            expert_back(l)

        def weights(t):
            at = tile(t)
            win[:, at] = dot_tn(rows[...], dg[:, at]).astype(BF16)
            wout[at, :] = dot_tn(act[:, at], dyrows[...]).astype(BF16)
        loop(FF // TILE, weights)
        pltpu.make_async_copy(win, R.gwin, rsem.at[OWIN]).start()
        pltpu.make_async_copy(wout, R.gwout, rsem.at[OWOUT]).start()

        got(R.er, DEXP)
        dn2 = dot(R.stmat[...], flat(R.er))
        dx, dgain = norm_back(R.hidden[...], R.gains[1:2, :], dn2)
        R.sm[...] = jnp.zeros((8, D), F32)
        R.sm[1:2, :] = dgain
        dh = g.astype(F32) + dx
        R.dh[...] = dh
        dattn = dh.astype(BF16)
        dmix = dot_nt(dattn, wo()).astype(BF16)
        dos = R.dos
        for u in range(24):
            at = 64 * (u // HEADS)
            h = 64 * (u % HEADS)
            dos[u, :, 0:64] = dmix[at:at + 32, h:h + 64]
            dos[u, :, 64:128] = dmix[at + 32:at + 64, h:h + 64]
        to_heads(dos, R.dor.at[l], DOUT + l)
        if l == 1:
            spread(R.rs, R.rr, RET, l)
        gout = dot_tn(R.mixed[...], dattn)
        R.gop[...] = gout.astype(BF16).reshape(16, 48, D)

        def reduce_out(i):
            push(R.gop.at[i], R.gor.at[s], GO, l, i, r)
        loop(SHARDS, reduce_out)

    def bwd_two(l):
        got(R.dkr, DQKV + l)
        dkr, dqkv, gp = R.dkr, R.dqkv, R.gp
        for u in range(24):
            at = 64 * (u // HEADS)
            h = 64 * (u % HEADS)
            dqkv[at:at + 64, D + h:D + h + 64] = dkr[u, 0:64, 0:64]
            dqkv[at:at + 64, 2 * D + h:2 * D + h + 64] = dkr[u, 0:64, 64:128]
            dqkv[at:at + 32, h:h + 64] = dkr[u, 64:96, 0:64]
            dqkv[at + 32:at + 64, h:h + 64] = dkr[u, 64:96, 64:128]
        nrm = R.nrm
        def part(t):
            at = slice(384 * t, 384 * t + 384)
            gp[:, :, :, at] = dot_tn(nrm[...], dqkv[:, at]).astype(BF16).reshape(4, 4, 48, 384)

        def reduce_a(i):
            push(gp.at[:, i, :, pl.ds(0, HALF)], R.r1a.at[z], RA1, l, y * 4 + i, r)

        def reduce_b(i):
            push(gp.at[i, :, :, pl.ds(HALF, HALF)], R.r1b.at[y], RB1, l, i * 4 + z, r)
        for t in range(3):
            part(t)
        loop(4, reduce_a)
        for t in range(3, 6):
            part(t)
        loop(4, reduce_b)
        dn = dot_nt(dqkv[:, 0:HALF], wa()) + dot_nt(dqkv[:, HALF:2 * HALF], wb())
        dx, dgain = norm_back(layer_in(l).astype(F32), R.gains[0:1, :], dn)
        low = (R.dh[...] + dx).astype(BF16)
        R.sgr[...] = low
        if l == 1:
            R.xsend[...] = low
            send(R.xsend, R.gin, GPASS, 0, s, r)
        R.sm[0:1, :] = dgain

        if l == 1:
            combine()

        def reduce_small(i):
            push(R.sm, R.smr.at[s], SMALL, l, i, r)
        loop(SHARDS, reduce_small)

    def reduce(l):
        r1a, r1b, r2a, r2b, gx, sx = (R.r1a, R.r1b, R.r2a, R.r2b, R.gx, R.sx)

        def four(ref, at):
            return ref[(0,) + at].astype(F32) + ref[(1,) + at].astype(F32) + ref[(2,) + at].astype(F32) + ref[(3,) + at].astype(F32)

        got(R.gor, GO)
        part = R.gor[0].astype(F32)
        for k in range(1, SHARDS):
            part = part + R.gor[k].astype(F32)
        R.gos[...] = part.astype(BF16)

        def out_over_replicas(i):
            push(R.gos, R.gox.at[r], GOX, c, s, i)
        loop(REPLICAS, out_over_replicas)

        got(r1a, RA1)
        got(r1b, RB1)
        for k in range(4):
            R.p2a[k] = four(r1a, (k,)).astype(BF16)
            R.p2b[k] = four(r1b, (k,)).astype(BF16)

        def reduce_two(i):
            push(R.p2a.at[i], r2a.at[y], RA2, l, i * 4 + z, r)
            push(R.p2b.at[i], r2b.at[z], RB2, l, y * 4 + i, r)
        loop(4, reduce_two)

        got(R.smr, SMALL)
        got(R.gtr, GTAB)
        small = R.smr[0]
        for k in range(1, SHARDS):
            small = small + R.smr[k]
        table = R.gtr[0]
        for k in range(1, 24):
            table = table + R.gtr[k]
        R.sxs[...] = small + jnp.concatenate([table, jnp.zeros((8, D - 128), F32)], axis=1)
        got(r2a, RA2)
        got(r2b, RB2)
        R.gxs[:, 0:HALF] = four(r2a, ()).astype(BF16)
        R.gxs[:, HALF:2 * HALF] = four(r2b, ()).astype(BF16)

        def over_replicas(i):
            push(R.gxs, gx.at[r], GX, c, s, i)
            push(R.sxs, sx.at[r], SX, c, s, i)
        loop(REPLICAS, over_replicas)
        got(R.gox, GOX)
        R.gout[...] = four(R.gox, ()).astype(BF16)
        got(gx, GX)
        got(sx, SX)
        R.gqkv[...] = four(gx, ()).astype(BF16)
        total = four(sx, ())
        mine = pltpu.roll(total, lax.rem(D - 48 * s, D), 1)
        R.ggain1[...] = mine[0:1, 0:48].astype(BF16)
        R.ggain2[...] = mine[1:2, 0:48].astype(BF16)
        rows = pltpu.roll(total[:, 0:128], lax.rem(128 - 2 * s, 128), 1)
        sent(mr.at[pl.ds(0, 31)], MISC)
        spare = R.misc
        for k in range(2):
            for h in range(HEADS):
                at = (h % 2) * 64 + k
                spare[k:k + 1, h:h + 1] = rows[2 + h // 2:3 + h // 2, at:at + 1]
        R.gtable[...] = spare[0:2, 0:HEADS].astype(BF16)

    for l in range(2):
        pl.when(c == l)(lambda l=l: fwd_one(l))
        if l == 0:
            pl.when((c == 0) & is_head)(set_heads)
        pl.when(is_head)(lambda l=l: head_fwd(l))
        if l == 0:
            set_routes()
            pl.when(c == 1)(lambda: send_dy(R.cot[...], 1))
        pl.when(c == l)(lambda l=l: fwd_two(l))
    for l in (1, 0):
        pl.when(c == l)(lambda l=l: bwd_one(l))
        pl.when(is_head)(lambda l=l: head_bwd(l))
        pl.when(c == l)(lambda l=l: bwd_two(l))
        pl.when(c == l)(lambda l=l: reduce(l))

    sent(ga.at[0, pl.ds(0, 3)], GA1)
    sent(gb.at[0, pl.ds(0, 3)], GB1)
    sent(ga.at[pl.ds(0, 3)], GA2)
    sent(gb.at[pl.ds(0, 3)], GB2)
    few = EXPERTS - 1
    sent(R.ds.at[pl.ds(0, few)], DISP)
    sent(R.rs.at[pl.ds(0, few)], RET)
    sent(R.ys.at[pl.ds(0, few)], DY)
    sent(R.es.at[pl.ds(0, few)], DEXP)
    sent(gw.at[pl.ds(0, 15)], GW)
    sent(R.gop.at[pl.ds(0, 15)], GO)
    sent(R.r1a.at[pl.ds(0, 3)], RA1)
    sent(R.r1b.at[pl.ds(0, 3)], RB1)
    sent(R.p2a.at[pl.ds(0, 3)], RA2)
    sent(R.p2b.at[pl.ds(0, 3)], RB2)
    sent(R.smr.at[pl.ds(0, 15)], SMALL)
    sent(R.gx.at[pl.ds(0, 3)], GX)
    sent(R.gox.at[pl.ds(0, 3)], GOX)
    sent(R.sx.at[pl.ds(0, 3)], SX)
    got(R.win, OWIN)
    got(R.wout, OWOUT)
    for l in range(2):
        @pl.when(c == l)
        def _():
            sent(R.xsend, XPASS if l == 0 else GPASS)
            for buf, i in ((R.qs, QKV + l), (R.dos, DOUT + l)):
                pl.when(is_head)(lambda buf=buf, i=i: sent(buf.at[pl.ds(0, 23)], i))
                pl.when(jnp.logical_not(is_head))(lambda buf=buf, i=i: sent(buf, i))

        @pl.when(is_head)
        def _():
            for buf, i in ((R.os, MIX + l), (R.dks, DQKV + l)):
                pl.when(c == l)(lambda buf=buf, i=i: sent(buf.at[l, pl.ds(0, 15)], i))
                pl.when(c != l)(lambda buf=buf, i=i: sent(buf.at[l], i))

    @pl.when(is_head)
    def _():
        sent(mr.at[pl.ds(0, 31)], GTAB)


def settle(*refs):
    ins, outs, held, sems = refs[:9], refs[9:18], refs[18:27], refs[27]
    pieces = [(i, pl.ds(0, ins[i].shape[0])) for i in range(7)]
    for i in (7, 8):
        step = ins[i].shape[0] // 6
        pieces += [(i, pl.ds(k * step, step)) for k in range(6)]
    into = [pltpu.make_async_copy(ins[i].at[at], held[i].at[at], sems.at[0, n]) for n, (i, at) in enumerate(pieces)]
    out = [pltpu.make_async_copy(held[i].at[at], outs[i].at[at], sems.at[1, n]) for n, (i, at) in enumerate(pieces)]
    for copy in into:
        copy.start()
    for first, second in zip(into, out):
        first.wait()
        second.start()
    for copy in out:
        copy.wait()


def body(tokens, cotangent, wqkv, wout, gain_attn, gain_ffn, rel_table, w_in, w_out_exp, expert_ids, gates, seg_ids, buckets):
    vmem = pl.BlockSpec(memory_space=pltpu.VMEM)
    hbm = pl.BlockSpec(memory_space=pl.ANY)
    shapes = ((TOK, D), (TOK, D), (48, 2304), (48, D), (1, 48), (1, 48), (2, HEADS), (D, FF), (FF, D))
    shapes = tuple(jax.ShapeDtypeStruct(v, BF16) for v in shapes)
    scratch = [pltpu.VMEM(*v) for v in SCRATCH.values()]
    outs = pl.pallas_call(
        kernel,
        out_shape=shapes,
        in_specs=[vmem] * 11 + [hbm] * 2,
        out_specs=(vmem,) * 7 + (hbm, hbm),
        scratch_shapes=scratch + [pltpu.SemaphoreType.DMA((34,)), pltpu.SemaphoreType.DMA((34,)), pltpu.SemaphoreType.REGULAR],
        compiler_params=pltpu.CompilerParams(has_side_effects=True, vmem_limit_bytes=64 * 1024 * 1024 - 65536),
        name="relay",
    )(tokens.reshape(TOK, D), cotangent.reshape(TOK, D), wqkv[0], wout[0], gain_attn, gain_ffn, rel_table[0],
      expert_ids.reshape(TOK, 2), gates.reshape(TOK, 2), seg_ids, buckets[None, :], w_in[0, 0], w_out_exp[0, 0])
    outs = pl.pallas_call(
        settle,
        out_shape=shapes,
        in_specs=[hbm] * 9,
        out_specs=(hbm,) * 9,
        scratch_shapes=[pltpu.VMEM(v.shape, BF16) for v in shapes] + [pltpu.SemaphoreType.DMA((2, 19))],
        compiler_params=pltpu.CompilerParams(vmem_limit_bytes=56 * 1024 * 1024),
        name="settle",
    )(*outs)
    acts, sgr, gqkv, gout, ggain1, ggain2, gtable, gwin, gwout = outs
    return (
        acts.reshape(1, 2, ROWS, D),
        sgr.reshape(1, 2, ROWS, D),
        gqkv[None],
        gout[None],
        ggain1,
        ggain2,
        gtable[None],
        gwin[None, None],
        gwout[None, None],
    )


def solution(mesh):
    in_specs = (
        P("replica", "shard", None),
        P("replica", "shard", None),
        P("section", "shard", None),
        P("section", "shard", None),
        P("section", "shard"),
        P("section", "shard"),
        P("section", "shard", None),
        P("section", ("shard", "replica"), None, None),
        P("section", ("shard", "replica"), None, None),
        P("section", "replica", "shard", None),
        P("section", "replica", "shard", None),
        P("replica", None),
        P(),
    )
    out_specs = (
        P("section", "replica", "shard", None),
        P("section", "replica", "shard", None),
        P("section", "shard", None),
        P("section", "shard", None),
        P("section", "shard"),
        P("section", "shard"),
        P("section", "shard", None),
        P("section", ("shard", "replica"), None, None),
        P("section", ("shard", "replica"), None, None),
    )
    return jax.shard_map(body, mesh=mesh, in_specs=in_specs, out_specs=out_specs, check_vma=False)
```
